32 devices in a mesh: seq: 8 (over y, x, core), mp: 4 (over z).
Axes of the slice: x: 2, y: 2, z: 4, core: 2. Of those that a mesh axis runs over, the one named last changes fastest.
Arguments:
- tokens: bfloat16 [8192, 2048], P('seq'), may hold values from -6 to 6
- cotangent: bfloat16 [8192, 2048], P('seq'), may hold values from -6 to 6
- destination: int32 [8192], replicated, may hold values from 0 to 8191, as said below
- lengths: int32 [6], replicated, may hold values from 1 to 2048, 8192 in all
- norm_gain: float32 [2048], replicated, may hold values from 0.1 to 1.9
- w_branch: bfloat16 [2048, 2736], P(None, 'mp'), may hold values from -0.125 to 0.125
- w_input: bfloat16 [2048, 2736], P(None, 'mp'), may hold values from -0.125 to 0.125
- conv_weight: float32 [4, 2736], P(None, 'mp'), may hold values from -3 to 3
- conv_bias: float32 [2736], P('mp'), may hold values from -3 to 3
- w_recur: bfloat16 [16, 171, 171], P('mp'), may hold values from -0.4375 to 0.4375
- w_ingate: bfloat16 [16, 171, 171], P('mp'), may hold values from -0.4375 to 0.4375
- decay_param: float32 [2736], P('mp'), may hold values from 3 to 9
- w_out: bfloat16 [2736, 2048], P('mp'), may hold values from -0.15625 to 0.15625
- mlp_gain: float32 [2048], replicated, may hold values from 0.1 to 1.9
- w_gate: bfloat16 [2048, 6144], P(None, 'mp'), may hold values from -0.125 to 0.125
- w_up: bfloat16 [2048, 6144], P(None, 'mp'), may hold values from -0.125 to 0.125
- w_down: bfloat16 [6144, 2048], P('mp'), may hold values from -0.15625 to 0.15625
Outputs:
- block_out: float32 [8192, 2048], P('seq', 'mp')
- input_grad: float32 [8192, 2048], P('seq', 'mp')
- grad_norm_gain: float32 [2048], P('mp')
- grad_w_branch: float32 [2048, 2736], P('seq', 'mp')
- grad_w_input: float32 [2048, 2736], P('seq', 'mp')
- grad_conv_weight: float32 [4, 2736], P(None, 'mp')
- grad_conv_bias: float32 [2736], P('mp')
- grad_w_recur: float32 [16, 171, 171], P('mp')
- grad_w_ingate: float32 [16, 171, 171], P('mp')
- grad_decay_param: float32 [2736], P('mp')
- grad_w_out: float32 [2736, 2048], P('mp', 'seq')
- grad_mlp_gain: float32 [2048], P('mp')
- grad_w_gate: float32 [2048, 6144], P('seq', 'mp')
- grad_w_up: float32 [2048, 6144], P('seq', 'mp')
- grad_w_down: float32 [6144, 2048], P('mp', 'seq')
The draws below stay inside these ranges and needn't reach their ends.
Inputs may be any that keep to these rules, and one draw needn't show every extreme that they name: destination is a permutation of the 8192 places; of the 1024 tokens in each aligned block of 1024 initial positions, exactly 128 go to each aligned block of 1024 places. The lengths sum to 8192, and the longest is exactly 2048.
All inputs are finite; a program needn't handle non-finite values.
Results may differ from the reference program's by a relative error of at most 0.0088.
Values may be sent and summed in bfloat16 or wider, within the bound.
No kernel may reach another device: no remote copies, remote signals or barrier semaphores. Data moves between devices by JAX's collectives and lax.ppermute only.
A program may use at most 320 MiB of HBM per device.

```python
import math
from functools import partial
import jax
import jax.numpy as jnp
import numpy as np
from jax import lax

D = 2048
FF = 6144
H = 16
BW = 171
CONV = 4
MAXLEN = 2048
TOK_DEV = 1024
R = 2736
TOKENS = 8192
NSEQ = 6


def draw_destination(key, part):
    key = jax.random.fold_in(key, 11)
    shard_count = TOKENS // TOK_DEV
    per_peer = TOK_DEV // shard_count
    source_key, landing_key = jax.random.split(key)
    source_order = jax.vmap(lambda subkey: jax.random.permutation(subkey, TOK_DEV))(jax.random.split(source_key, shard_count)).astype(jnp.int32)
    landing = jax.vmap(lambda subkey: jax.random.permutation(subkey, TOK_DEV))(jax.random.split(landing_key, shard_count)).astype(jnp.int32)
    blocks = landing.reshape(shard_count, shard_count, per_peer).transpose(1, 0, 2)
    block_base = (jnp.arange(shard_count, dtype=jnp.int32) * TOK_DEV)[None, :, None]
    targets = (blocks + block_base).reshape(shard_count, TOK_DEV)
    placed = jax.vmap(lambda row_slots, row_values: jnp.zeros((TOK_DEV,), jnp.int32).at[row_slots].set(row_values))(source_order, targets)
    return placed.reshape(TOKENS)


def block_levels(rng, shape, shards, least, high):
    level, own = 1.0, jax.random.fold_in(rng, 6)
    for position, shards_of in shards:
        heights = jnp.exp(jax.random.uniform(jax.random.fold_in(own, position), (shards_of,), jnp.float32, least / len(shards), high / len(shards)))
        level = level * jnp.repeat(heights, shape[position] // shards_of).reshape([-1 if axis == position else 1 for axis in range(len(shape))])
    return level


def profile(number_of, total, most, skew):
    portions = [(1 << 20) // math.isqrt(grade ** skew) + 1 for grade in range(2, number_of + 1)]
    surplus, given = total - most - (number_of - 1), [1] * (number_of - 1)
    while surplus > 0:
        movable = [i for i in range(number_of - 1) if given[i] < most]
        whole, left = sum([portions[i] for i in movable]), surplus
        for i in movable:
            addition = min(most - given[i], max(1, left * portions[i] // whole), surplus)
            given[i] = given[i] + addition
            surplus = surplus - addition
    return np.array([most] + given)


def uneven(rng, number_of, total, limit, skew):
    if number_of == 2:
        one = jax.random.randint(rng, (), max(1, total - limit), min(limit, total - 1) + 1)
        return jnp.stack([one, total - one])
    sizes = jnp.asarray(profile(number_of, total, limit, skew), jnp.int32)
    twos = (number_of - 1) // 2
    source_of, sink = sizes[1:1 + 2 * twos:2], sizes[2:2 + 2 * twos:2]
    room = jnp.minimum(source_of - 1, limit - sink)
    moved = jax.random.randint(jax.random.fold_in(rng, 1), (twos,), 0, 1 << 20) % (room + 1)
    sizes = sizes.at[1:1 + 2 * twos:2].set(source_of - moved).at[2:2 + 2 * twos:2].set(sink + moved)
    return sizes[jax.random.permutation(jax.random.fold_in(rng, 2), number_of)]


def gaussian(stream_key, dims, scale, most, cuts=(), kind=jnp.bfloat16):
    drawn = jax.random.normal(stream_key, dims, jnp.float32) * scale
    if len(cuts) > 0:
        drawn = block_levels(stream_key, dims, cuts, -0.22, 0.18) * drawn
    return jnp.clip(drawn, min=-most, max=most).astype(kind)


def setup_inputs(seed: int = 0) -> dict:
    arg_keys = jax.random.split(jax.random.key(seed), 18)
    tokens = gaussian(arg_keys[0], (TOKENS, D), 1.0, 6.0, ((0, 8),))
    cotangent = gaussian(arg_keys[1], (TOKENS, D), 1.0, 6.0, ((0, 8),))
    destination = draw_destination(jax.random.fold_in(arg_keys[17], 71), 0)
    lengths = uneven(arg_keys[3], NSEQ, TOKENS, MAXLEN, 2).astype(jnp.int32)
    norm_gain = jnp.clip(1.0 + 0.18 * jax.random.normal(arg_keys[4], (D,), jnp.float32), 0.1, 1.9)
    w_branch = gaussian(arg_keys[5], (D, R), D ** -0.5, 0.125, ((1, 4),))
    w_input = gaussian(arg_keys[6], (D, R), D ** -0.5, 0.125, ((1, 4),))
    conv_weight = gaussian(arg_keys[7], (CONV, R), 0.5, 3.0, ((1, 4),), jnp.float32)
    conv_bias = gaussian(arg_keys[8], (R,), 0.5, 3.0, ((0, 4),), jnp.float32)
    w_recur = gaussian(arg_keys[9], (H, BW, BW), BW ** -0.5, 0.4375, ((0, 4),))
    w_ingate = gaussian(arg_keys[10], (H, BW, BW), BW ** -0.5, 0.4375, ((0, 4),))
    decay_param = jnp.clip(3.0 + 6.0 * jax.random.uniform(arg_keys[11], (R,), jnp.float32) ** block_levels(arg_keys[11], (R,), ((0, 4),), -0.2, 0.2), 3.0, 9.0)
    w_out = gaussian(arg_keys[12], (R, D), (R // 2) ** -0.5, 0.15625, ((0, 4),))
    mlp_gain = jnp.clip(1.0 + 0.18 * jax.random.normal(arg_keys[13], (D,), jnp.float32), 0.1, 1.9)
    w_gate = gaussian(arg_keys[14], (D, FF), D ** -0.5, 0.125, ((1, 4),))
    w_up = gaussian(arg_keys[15], (D, FF), D ** -0.5, 0.125, ((1, 4),))
    w_down = gaussian(arg_keys[16], (FF, D), (FF // 4) ** -0.5, 0.15625, ((0, 4),))
    return dict(tokens=tokens, cotangent=cotangent, destination=destination, lengths=lengths, norm_gain=norm_gain, w_branch=w_branch, w_input=w_input, conv_weight=conv_weight, conv_bias=conv_bias, w_recur=w_recur, w_ingate=w_ingate, decay_param=decay_param, w_out=w_out, mlp_gain=mlp_gain, w_gate=w_gate, w_up=w_up, w_down=w_down)


@jax.custom_vjp
def low(v):
    return lax.optimization_barrier(v.astype(jnp.bfloat16)).astype(jnp.float32)

@jax.custom_vjp
def low_back(v):
    return v

def low_keep(v):
    return (low(v), None)

def low_pass(kept, grad):
    return (grad,)

def back_keep(v):
    return (v, None)

def back_low(kept, grad):
    return (low(grad),)
low.defvjp(low_keep, low_pass)
low_back.defvjp(back_keep, back_low)
EPSILON = 1e-06
GATE_POWER = 8.0
ROOT_FLOOR = 0.01
HIGHEST_MODE = lax.Precision.HIGHEST

def norm_rows(values, gain):
    return values * lax.rsqrt(lax.optimization_barrier(jnp.mean(values * values, axis=-1, keepdims=True)) + EPSILON) * gain

def product(left, right):
    return jnp.dot(left, right, precision=HIGHEST_MODE, preferred_element_type=jnp.float32)

def chain(first, second):
    return (first[0] * second[0], second[0] * first[1] + second[1])

def gates(recur, ingate, convolved, decay_param, notstart):
    reset_gate = jax.nn.sigmoid(recur)
    input_gate = jax.nn.sigmoid(ingate)
    keep_rate = jnp.exp(-GATE_POWER * reset_gate * jax.nn.softplus(-decay_param))
    drive_term = jnp.sqrt(1.0 - keep_rate * keep_rate + ROOT_FLOOR) * (input_gate * convolved)
    return (keep_rate * notstart, drive_term)

def block(source_rows, destination, positions, seq_start, notstart, tokens, norm_gain, w_branch, w_input, conv_weight, conv_bias, w_recur, w_ingate, decay_param, w_out, mlp_gain, w_gate, w_up, w_down):
    stream = tokens[source_rows]
    hidden = low(norm_rows(stream, norm_gain))
    branch = low_back(product(hidden, w_branch))
    inputs = low_back(product(hidden, w_input))
    convolved = conv_bias + conv_weight[0] * inputs
    for offset in range(1, CONV):
        shifted = jnp.pad(inputs, ((offset, 0), (0, 0)))[:-offset]
        in_sequence = (positions - offset >= seq_start).astype(jnp.float32)[:, None]
        convolved = convolved + conv_weight[offset] * shifted * in_sequence
    convolved = low(convolved)
    blocked = convolved.reshape(-1, H, BW)
    recur = low_back(jnp.einsum('thb,hbe->the', blocked, w_recur, precision=HIGHEST_MODE).reshape(-1, H * BW))
    ingate = low_back(jnp.einsum('thb,hbe->the', blocked, w_ingate, precision=HIGHEST_MODE).reshape(-1, H * BW))
    keep_rate, drive_term = gates(recur, ingate, convolved, decay_param, notstart)
    _, states = lax.associative_scan(chain, (keep_rate, drive_term))
    mixed = low(states * jax.nn.gelu(branch))
    resid = stream + low_back(product(mixed, w_out))
    normed = low(norm_rows(resid, mlp_gain))
    gate_pre = low_back(product(normed, w_gate))
    up_pre = low_back(product(normed, w_up))
    inner_act = low(jax.nn.gelu(gate_pre) * up_pre)
    result = resid + low_back(product(inner_act, w_down))
    return result[destination]

def reference(tokens, cotangent, destination, lengths, norm_gain, w_branch, w_input, conv_weight, conv_bias, w_recur, w_ingate, decay_param, w_out, mlp_gain, w_gate, w_up, w_down):
    total_rows = tokens.shape[0]
    positions = jnp.arange(total_rows, dtype=jnp.int32)
    source_rows = jnp.zeros((total_rows,), jnp.int32).at[destination].set(positions)
    seq_starts = (jnp.cumsum(lengths) - lengths).astype(jnp.int32)
    seq_start = lax.optimization_barrier(jnp.max(jnp.where(seq_starts[None, :] <= positions[:, None], seq_starts[None, :], 0), axis=1)).astype(jnp.int32)
    notstart = (positions > seq_start).astype(jnp.float32)[:, None]
    params = (norm_gain, w_branch, w_input, conv_weight, conv_bias, w_recur, w_ingate, decay_param, w_out, mlp_gain, w_gate, w_up, w_down)
    params = tuple((item.astype(jnp.float32) for item in params))
    apply_block = partial(block, source_rows, destination, positions, seq_start, notstart)
    result, pullback = jax.vjp(apply_block, tokens.astype(jnp.float32), *params)
    gradients = pullback(cotangent.astype(jnp.float32))
    return (result, gradients[0], gradients[1], gradients[2], gradients[3], gradients[4], gradients[5], gradients[6], gradients[7], gradients[8], gradients[9], gradients[10], gradients[11], gradients[12], gradients[13])
```

```python
import functools

import jax
import jax.numpy as jnp
import numpy as np
from jax import lax
from jax.experimental import pallas as pl
from jax.experimental.pallas import tpu as pltpu
from jax.sharding import PartitionSpec as P

CONV = 4
EPSILON = 1e-06
GATE_POWER = 8.0
ROOT_FLOOR = 0.01
LANES = 128
GROUP = 8
CHUNKS = 2
F32 = jnp.float32
BF16 = jnp.bfloat16
MIB = 1 << 20
GELU_A = 0.7978845608028654
GELU_B = 0.044715

NN = (((1,), (0,)), ((), ()))
NT = (((1,), (1,)), ((), ()))
TN = (((0,), (0,)), ((), ()))


def mm(left, right, dims=NN):
    return lax.dot_general(left, right, dims, preferred_element_type=F32)


def call(body, grid, in_specs, out_specs, out_shape, scratch=(), prefetch=0, aliases=None, flops=0, moved=0):
    return pl.pallas_call(
        body,
        grid_spec=pltpu.PrefetchScalarGridSpec(
            num_scalar_prefetch=prefetch,
            grid=grid,
            in_specs=in_specs,
            out_specs=out_specs,
            scratch_shapes=list(scratch),
        ),
        out_shape=out_shape,
        input_output_aliases=aliases or {},
        compiler_params=pltpu.CompilerParams(
            dimension_semantics=("arbitrary",) * len(grid), vmem_limit_bytes=60 * MIB
        ),
        cost_estimate=pl.CostEstimate(flops=flops, bytes_accessed=moved, transcendentals=0),
    )


def whole(shape):
    zeros = (0,) * len(shape)
    return pl.BlockSpec(shape, lambda *_: zeros)


def struct(shape, dtype):
    return jax.ShapeDtypeStruct(shape, dtype)


def sigmoid(x):
    return 0.5 * jnp.tanh(0.5 * x) + 0.5


def gelu(x):
    return 0.5 * x * (1.0 + jnp.tanh(GELU_A * (x + GELU_B * x * x * x)))


def gelu_both(x):
    square = x * x
    t = jnp.tanh(GELU_A * x * (1.0 + GELU_B * square))
    half = 0.5 * (1.0 + t)
    slope = half + 0.5 * x * (1.0 - t * t) * (GELU_A * (1.0 + 3.0 * GELU_B * square))
    return x * half, slope


def softplus_neg(x):
    return jnp.log1p(jnp.exp(-jnp.abs(x))) + jnp.maximum(-x, 0.0)


def one_hot(rows, lanes):
    return jnp.where(rows == lanes, 1.0, 0.0).astype(BF16)


def send_order(turn, dest_row, dest_col, values):
    rows, width = values.shape
    tile = 256

    def body(turn_ref, row_ref, col_ref, val_ref, out_ref, rank_ref):
        i = pl.program_id(0)

        @pl.when(i == 0)
        def _():
            before = jnp.where(col_ref[...] < row_ref[...], 1.0, 0.0)
            rank = jnp.sum(before, axis=0, keepdims=True).astype(jnp.int32)
            rank_ref[...] = rank ^ turn_ref[0]

        place = lax.broadcasted_iota(jnp.int32, (tile, rows), 0) + i * tile
        out_ref[...] = mm(one_hot(place, rank_ref[...]), val_ref[...]).astype(BF16)

    return call(
        body,
        (rows // tile,),
        [whole((1, rows)), whole((rows, 1)), whole((rows, width))],
        pl.BlockSpec((tile, width), lambda i, *_: (i, 0)),
        struct((rows, width), BF16),
        [pltpu.VMEM((1, rows), jnp.int32)],
        prefetch=1,
        flops=2 * rows * rows * width,
        moved=4 * rows * width,
    )(turn, dest_row, dest_col, values)


def place_rows(place_col, landing_row, values):
    rows, width = values.shape
    tile = 256

    def body(place_ref, land_ref, val_ref, out_ref):
        out_ref[...] = mm(one_hot(place_ref[...], land_ref[...]), val_ref[...]).astype(out_ref.dtype)

    return call(
        body,
        (rows // tile,),
        [pl.BlockSpec((tile, 1), lambda i: (i, 0)), whole((1, rows)), whole((rows, width))],
        pl.BlockSpec((tile, width), lambda i: (i, 0)),
        struct((rows, width), BF16),
        flops=2 * rows * rows * width,
        moved=4 * rows * width,
    )(place_col, landing_row, values)


def split_columns(near_ref, far_ref, values, parity, parts):
    size = values.shape[1] // parts
    for q in range(parts // 2):
        to = slice(q * size, (q + 1) * size)
        even = values[:, 2 * q * size : (2 * q + 1) * size]
        odd = values[:, (2 * q + 1) * size : (2 * q + 2) * size]
        near_ref[:, to] = jnp.where(parity == 0, even, odd)
        far_ref[:, to] = jnp.where(parity == 0, odd, even)


def place_upstream(place, place_col, landing_row, blocks, parts):
    count = len(blocks)
    size, width = blocks[0].shape
    rows = count * size
    tile = 256

    def body(my_ref, place_ref, land_ref, *refs):
        out_ref, near_ref, far_ref, val_ref, sem = refs[count:]

        @pl.when(pl.program_id(0) == 0)
        def _():
            copies = [
                pltpu.make_async_copy(refs[k], val_ref.at[k * size : (k + 1) * size], sem.at[k])
                for k in range(count)
            ]
            for copy in copies:
                copy.start()
            for copy in copies:
                copy.wait()

        moved = mm(one_hot(place_ref[...], land_ref[...]), val_ref[...])
        out_ref[...] = moved.astype(BF16)
        split_columns(near_ref, far_ref, moved.astype(BF16), my_ref[2], parts)

    return call(
        body,
        (rows // tile,),
        [pl.BlockSpec((tile, 1), lambda i, *_: (i, 0)), whole((1, rows))]
        + [pl.BlockSpec(memory_space=pl.ANY)] * count,
        [
            pl.BlockSpec((tile, width), lambda i, *_: (i, 0)),
            pl.BlockSpec((tile, width // 2), lambda i, *_: (i, 0)),
            pl.BlockSpec((tile, width // 2), lambda i, *_: (i, 0)),
        ],
        [
            struct((rows, width), BF16),
            struct((rows, width // 2), BF16),
            struct((rows, width // 2), BF16),
        ],
        [pltpu.VMEM((rows, width), BF16), pltpu.SemaphoreType.DMA((count,))],
        prefetch=1,
        flops=2 * rows * rows * width,
        moved=6 * rows * width,
    )(place, place_col, landing_row, *blocks)


def restore_rows(dest_row, dest_col, values):
    rows, width = values.shape
    tile = 256

    def body(row_ref, col_ref, val_ref, out_ref):
        before = jnp.where(row_ref[...] < col_ref[...], 1.0, 0.0)
        rank = jnp.sum(before, axis=1, keepdims=True).astype(jnp.int32)
        spot = lax.broadcasted_iota(jnp.int32, (tile, rows), 1)
        out_ref[...] = mm(one_hot(spot, rank), val_ref[...])

    return call(
        body,
        (rows // tile,),
        [whole((1, rows)), pl.BlockSpec((tile, 1), lambda i: (i, 0)), whole((rows, width))],
        pl.BlockSpec((tile, width), lambda i: (i, 0)),
        struct((rows, width), F32),
        flops=2 * rows * rows * width,
        moved=6 * rows * width,
    )(dest_row, dest_col, values)


def project(place, landing_row, arrived, gain, weights, parts):
    rows, width = arrived.shape
    wide = weights.shape[1]
    half = wide // 2
    tile = 256

    def body(
        my_ref, land_ref, arr_ref, gain_ref, w_ref, stream_ref, near_ref, far_ref, branch_ref, inputs_ref
    ):
        i = pl.program_id(0)
        place = lax.broadcasted_iota(jnp.int32, (tile, rows), 0) + i * tile
        x = mm(one_hot(place, land_ref[...]), arr_ref[...])
        stream_ref[...] = x.astype(BF16)
        inv = lax.rsqrt(jnp.mean(x * x, axis=-1, keepdims=True) + EPSILON)
        hidden = (x * inv * gain_ref[...]).astype(BF16)
        split_columns(near_ref, far_ref, hidden, my_ref[2], parts)
        branch_ref[...] = mm(hidden, w_ref[:, :half])
        inputs_ref[...] = mm(hidden, w_ref[:, half:])

    return call(
        body,
        (rows // tile,),
        [whole((1, rows)), whole((rows, width)), whole((1, width)), whole((width, wide))],
        [
            pl.BlockSpec((tile, width), lambda i, *_: (i, 0)),
            pl.BlockSpec((tile, width // 2), lambda i, *_: (i, 0)),
            pl.BlockSpec((tile, width // 2), lambda i, *_: (i, 0)),
            pl.BlockSpec((tile, half), lambda i, *_: (i, 0)),
            pl.BlockSpec((tile, half), lambda i, *_: (i, 0)),
        ],
        [
            struct((rows, width), BF16),
            struct((rows, width // 2), BF16),
            struct((rows, width // 2), BF16),
            struct((rows, half), F32),
            struct((rows, half), F32),
        ],
        prefetch=1,
        flops=2 * rows * width * (rows + wide),
        moved=6 * rows * width + 2 * width * wide + 4 * rows * wide,
    )(place, landing_row, arrived, gain, weights)


def tile_scan(rates, drives, keep_in, state_in, reverse):
    rows, lanes = rates.shape
    groups = rows // GROUP
    a = rates.reshape(groups, GROUP, lanes)
    d = drives.reshape(groups, GROUP, lanes)
    spot = lax.broadcasted_iota(jnp.int32, (groups, GROUP, lanes), 1)
    for by in (1, 2, 4):
        turn = GROUP - by if reverse else by
        ok = spot < GROUP - by if reverse else spot >= by
        d_near = pltpu.roll(d, turn, 1)
        a_near = pltpu.roll(a, turn, 1)
        d = jnp.where(ok, a * d_near + d, d)
        a = jnp.where(ok, a * a_near, a)
    end = 0 if reverse else GROUP - 1
    keeps, states = [None] * groups, [None] * groups
    for g in range(groups - 1, -1, -1) if reverse else range(groups):
        keeps[g] = a[g] * keep_in
        states[g] = d[g] + a[g] * state_in
        keep_in = keeps[g][end : end + 1]
        state_in = states[g][end : end + 1]
    return jnp.concatenate(keeps, 0), jnp.concatenate(states, 0), keep_in, state_in


def recurrent_forward(inputs, halo, dist, conv_weight, conv_bias, decay, gate_weights):
    rows, width = inputs.shape
    tile = 256
    last = rows // tile - 1

    def body(
        in_ref, halo_ref, dist_ref, cw_ref, cb_ref, dp_ref, gw_ref,
        conv_ref, pre_ref, keep_ref, prefix_ref, local_ref, tail_ref,
        ext, carry,
    ):
        i = pl.program_id(0)

        @pl.when(i == 0)
        def _():
            ext[0:8] = halo_ref[...]
            carry[0:1] = jnp.ones((1, width), F32)
            carry[1:2] = jnp.zeros((1, width), F32)

        @pl.when(i > 0)
        def _():
            ext[0:8] = ext[tile : tile + 8]

        ext[8 : 8 + tile] = in_ref[...]
        dist = dist_ref[...]
        conv = cb_ref[...] + cw_ref[0:1] * ext[8 : 8 + tile]
        for k in range(1, CONV):
            conv = conv + jnp.where(dist >= k, cw_ref[k : k + 1] * ext[8 - k : 8 - k + tile], 0.0)
        conv_low = conv.astype(BF16)
        conv_ref[...] = conv_low
        pre_ref[...] = mm(conv_low, gw_ref[...])
        notstart = dist > 0
        for lane in range(0, width, LANES):
            cut = slice(lane, lane + LANES)
            far = slice(width + lane, width + lane + LANES)
            reset = sigmoid(pre_ref[:, cut])
            gate = sigmoid(pre_ref[:, far])
            keep = jnp.exp((-GATE_POWER * softplus_neg(dp_ref[:, cut])) * reset)
            drive = jnp.sqrt(1.0 - keep * keep + ROOT_FLOOR) * (gate * conv_ref[:, cut].astype(F32))
            rate = jnp.where(notstart, keep, 0.0)
            keep_ref[:, cut] = rate
            keeps, states, keep_out, state_out = tile_scan(
                rate, drive, carry[0:1, cut], carry[1:2, cut], False
            )
            prefix_ref[:, cut] = keeps
            local_ref[:, cut] = states
            carry[0:1, cut] = keep_out
            carry[1:2, cut] = state_out

        @pl.when(i == last)
        def _():
            tail_ref[...] = carry[...]

    tiles = pl.BlockSpec((tile, width), lambda i: (i, 0))
    return call(
        body,
        (rows // tile,),
        [
            tiles,
            whole((8, width)),
            pl.BlockSpec((tile, 1), lambda i: (i, 0)),
            whole((CONV, width)),
            whole((1, width)),
            whole((1, width)),
            whole((width, 2 * width)),
        ],
        [
            tiles,
            pl.BlockSpec((tile, 2 * width), lambda i: (i, 0)),
            tiles,
            tiles,
            tiles,
            whole((8, width)),
        ],
        [
            struct((rows, width), BF16),
            struct((rows, 2 * width), F32),
            struct((rows, width), F32),
            struct((rows, width), F32),
            struct((rows, width), F32),
            struct((8, width), F32),
        ],
        [pltpu.VMEM((tile + 8, width), F32), pltpu.VMEM((8, width), F32)],
        flops=4 * rows * width * width + 200 * rows * width,
        moved=30 * rows * width,
    )(inputs, halo, dist, conv_weight, conv_bias, decay, gate_weights)


def finish_states(place, pieces, local, prefix, branch, owners):
    rows, width = local.shape
    shards = pieces.shape[0]
    tile = rows // owners // CHUNKS

    def body(my_ref, pieces_ref, local_ref, prefix_ref, branch_ref, states_ref, mixed_ref, carry_ref):
        mine = my_ref[0]

        @pl.when(pl.program_id(0) == 0)
        def _():
            entering = jnp.zeros((1, width), F32)
            for s in range(shards - 1):
                longer = pieces_ref[s, 0:1] * entering + pieces_ref[s, 1:2]
                entering = jnp.where(s < mine, longer, entering)
            carry_ref[...] = jnp.broadcast_to(entering, (8, width))

        states = local_ref[...] + prefix_ref[...] * carry_ref[0:1]
        states_ref[...] = states
        mixed_ref[0, 0] = (states * gelu(branch_ref[...])).astype(BF16)

    tiles = pl.BlockSpec((tile, width), lambda i, *_: (i, 0))
    return call(
        body,
        (rows // tile,),
        [whole(pieces.shape), tiles, tiles, tiles],
        [
            tiles,
            pl.BlockSpec((1, 1, tile, width), lambda i, *_: (i % CHUNKS, i // CHUNKS, 0, 0)),
            whole((8, width)),
        ],
        [
            struct((rows, width), F32),
            struct((CHUNKS, owners, tile, width), BF16),
            struct((8, width), F32),
        ],
        prefetch=1,
        flops=60 * rows * width,
        moved=18 * rows * width,
    )(place, pieces, local, prefix, branch)


def output_rows(chunk, place, mixed_full, w_near, w_far, stream, gain):
    sources, own, width = mixed_full.shape
    model = stream.shape[1]
    half = model // 2

    def body(place_ref, mixed_ref, near_ref, far_ref, stream_ref, gain_ref, resid_ref, normed_ref):
        s = pl.program_id(0)
        near = pl.ds(pl.multiple_of(place_ref[2] * half, half), half)
        far = pl.ds(pl.multiple_of((1 - place_ref[2]) * half, half), half)

        @pl.when(s == 0)
        def _():
            resid_ref[...] = stream_ref[...].astype(F32)

        resid_ref[:, near] += mm(mixed_ref[0], near_ref[0])
        resid_ref[:, far] += mm(mixed_ref[0], far_ref[0])

        @pl.when(s == sources - 1)
        def _():
            x = resid_ref[...]
            inv = lax.rsqrt(jnp.mean(x * x, axis=-1, keepdims=True) + EPSILON)
            normed_ref[...] = (x * inv * gain_ref[...]).astype(BF16)

    return call(
        body,
        (sources,),
        [
            pl.BlockSpec((1, own, width), lambda s, *_: (s, 0, 0)),
            pl.BlockSpec((1, width, half), lambda s, *_: (s, 0, 0)),
            pl.BlockSpec((1, width, half), lambda s, *_: (s, 0, 0)),
            pl.BlockSpec((own, model), lambda s, p: (p[1] * CHUNKS + chunk, 0)),
            whole((1, model)),
        ],
        [whole((own, model)), whole((own, model))],
        [struct((own, model), F32), struct((own, model), BF16)],
        prefetch=1,
        flops=2 * sources * own * width * model,
        moved=2 * sources * width * model + 8 * own * model,
    )(place, mixed_full, w_near, w_far, stream, gain)


def mlp_chunk(chunk, place, normed, upstream, resid_own, w_gate, w_up, w_down, parts, kept):
    rows, model = normed.shape
    hidden = w_gate.shape[1]
    total = upstream.shape[0]
    sub = resid_own.shape[0]
    tile = 256 if hidden % 256 == 0 else LANES
    steps = hidden // tile

    def body(place_ref, n_ref, u_ref, r_ref, wg_ref, wu_ref, wd_ref, *rest):
        act_ref, gate_ref, up_ref, near_ref, far_ref, down_ref, grad_ref, down_acc, grad_acc = rest[-9:]
        s = pl.program_id(0)

        @pl.when(s == 0)
        def _():
            split_columns(near_ref, far_ref, n_ref[...], place_ref[2], parts)
            down_acc[...] = jnp.zeros_like(down_acc)
            own = pl.ds(pl.multiple_of(place_ref[1] * sub, sub), sub)
            down_acc[own, :] = r_ref[...]

        gate_pre = mm(n_ref[...], wg_ref[...])
        up_pre = mm(n_ref[...], wu_ref[...])
        inner = mm(u_ref[...], wd_ref[...], NT)
        act, slope = gelu_both(gate_pre)
        inner_act = (act * up_pre).astype(BF16)
        gate_low = (inner * up_pre * slope).astype(BF16)
        up_low = (inner * act).astype(BF16)
        act_ref[...] = inner_act
        gate_ref[...] = gate_low
        up_ref[...] = up_low
        down_acc[...] += mm(inner_act, wd_ref[...])
        both = mm(gate_low, wg_ref[...], NT) + mm(up_low, wu_ref[...], NT)

        @pl.when(s == 0)
        def _():
            grad_acc[...] = both

        @pl.when(s > 0)
        def _():
            grad_acc[...] += both

        @pl.when(s == steps - 1)
        def _():
            down_ref[...] = down_acc[...].astype(BF16)
            grad_ref[...] = grad_acc[...].astype(BF16)

    slots = pl.BlockSpec((rows, tile), lambda s, *_: (chunk, s))
    any_spec = pl.BlockSpec(memory_space=pl.ANY)
    kept = tuple(kept)
    return call(
        body,
        (steps,),
        [
            whole((rows, model)),
            pl.BlockSpec((rows, model), lambda s, *_: (chunk, 0)),
            whole((sub, model)),
            pl.BlockSpec((model, tile), lambda s, *_: (0, s)),
            pl.BlockSpec((model, tile), lambda s, *_: (0, s)),
            pl.BlockSpec((tile, model), lambda s, *_: (s, 0)),
        ]
        + [any_spec] * len(kept),
        [
            slots,
            slots,
            slots,
            pl.BlockSpec((rows, model // 2), lambda s, *_: (chunk, 0)),
            pl.BlockSpec((rows, model // 2), lambda s, *_: (chunk, 0)),
            pl.BlockSpec((rows, model), lambda s, *_: (chunk, 0)),
            whole((rows, model)),
        ],
        [
            struct((total, hidden), BF16),
            struct((total, hidden), BF16),
            struct((total, hidden), BF16),
            struct((total, model // 2), BF16),
            struct((total, model // 2), BF16),
            struct((total, model), BF16),
            struct((rows, model), BF16),
        ],
        [pltpu.VMEM((rows, model), F32), pltpu.VMEM((rows, model), F32)],
        prefetch=1,
        aliases={7 + j: j for j in range(len(kept))},
        flops=12 * rows * hidden * model,
        moved=6 * hidden * model + 10 * rows * model,
    )(place, normed, upstream, resid_own, w_gate, w_up, w_down, *kept)


def resid_backward(chunk, place, normed_grad, upstream, resid_own, gain, w_near, w_far):
    own, model = resid_own.shape
    sources, width, half = w_near.shape

    def body(place_ref, g_ref, up_ref, r_ref, gain_ref, near_ref, far_ref, rg_ref, low_ref, mg_ref, sum_ref):
        @pl.when(pl.program_id(0) == 0)
        def _():
            x = r_ref[...]
            g = g_ref[...].astype(F32)
            inv = lax.rsqrt(jnp.mean(x * x, axis=-1, keepdims=True) + EPSILON)
            unit = x * inv
            scaled = g * gain_ref[...]
            dot = jnp.mean(scaled * unit, axis=-1, keepdims=True)
            grad = up_ref[...].astype(F32) + inv * (scaled - unit * dot)
            rg_ref[...] = grad
            low_ref[...] = grad.astype(BF16)
            sum_ref[...] = jnp.sum(g * unit, axis=0, keepdims=True)

        near = pl.ds(pl.multiple_of(place_ref[2] * half, half), half)
        far = pl.ds(pl.multiple_of((1 - place_ref[2]) * half, half), half)
        mg_ref[0] = (mm(low_ref[:, near], near_ref[0], NT) + mm(low_ref[:, far], far_ref[0], NT)).astype(BF16)

    rows = whole((own, model))
    return call(
        body,
        (sources,),
        [
            rows,
            pl.BlockSpec((own, model), lambda s, p: (chunk * sources + p[1], 0)),
            rows,
            whole((1, model)),
            pl.BlockSpec((1, width, half), lambda s, *_: (s, 0, 0)),
            pl.BlockSpec((1, width, half), lambda s, *_: (s, 0, 0)),
        ],
        [rows, rows, pl.BlockSpec((1, own, width), lambda s, *_: (s, 0, 0)), whole((1, model))],
        [
            struct((own, model), F32),
            struct((own, model), BF16),
            struct((sources, own, width), BF16),
            struct((1, model), F32),
        ],
        prefetch=1,
        flops=2 * sources * own * width * model,
        moved=2 * sources * width * model + 14 * own * model,
    )(place, normed_grad, upstream, resid_own, gain, w_near, w_far)


def recurrent_back_scan(mixed_grads, branch, keep, tail):
    rows, width = branch.shape
    owners, sub = mixed_grads[0].shape[:2]
    tile = sub * CHUNKS
    tiles_n = owners

    def body(*refs):
        parts = refs[:CHUNKS]
        branch_ref, keep_ref, tail_ref, grad_ref, after_ref, edge_ref, mg_ref, ext, carry = refs[CHUNKS:]
        i = pl.program_id(0)
        for c in range(CHUNKS):
            mg_ref[c * sub : (c + 1) * sub] = parts[c][0]

        @pl.when(i == 0)
        def _():
            ext[tile : tile + 8] = jnp.ones((8, width), F32)
            carry[0:1] = jnp.ones((1, width), F32)
            carry[1:2] = jnp.zeros((1, width), F32)

        @pl.when(i > 0)
        def _():
            ext[tile : tile + 8] = ext[0:8]

        ext[0:tile] = keep_ref[...]
        for lane in range(0, width, LANES):
            cut = slice(lane, lane + LANES)
            direct = mg_ref[:, cut].astype(F32) * gelu(branch_ref[:, cut])
            keeps, grads, keep_out, grad_out = tile_scan(
                ext[1 : tile + 1, cut], direct, carry[0:1, cut], carry[1:2, cut], True
            )
            grad_ref[:, cut] = grads
            after_ref[:, cut] = keeps
            carry[0:1, cut] = keep_out
            carry[1:2, cut] = grad_out

        @pl.when(i == tiles_n - 1)
        def _():
            edge_ref[0:1] = tail_ref[0:1]
            edge_ref[1:2] = keep_ref[0:1] * carry[1:2]
            edge_ref[2:8] = jnp.zeros((6, width), F32)

    tiles = pl.BlockSpec((tile, width), lambda i: (tiles_n - 1 - i, 0))
    return call(
        body,
        (tiles_n,),
        [pl.BlockSpec((1, sub, width), lambda i: (tiles_n - 1 - i, 0, 0))] * CHUNKS
        + [tiles, tiles, whole((8, width))],
        [tiles, tiles, whole((8, width)), tiles],
        [
            struct((rows, width), F32),
            struct((rows, width), F32),
            struct((8, width), F32),
            struct((rows, width), BF16),
        ],
        [pltpu.VMEM((tile + 8, width), F32), pltpu.VMEM((8, width), F32)],
        flops=100 * rows * width,
        moved=18 * rows * width,
    )(*mixed_grads, branch, keep, tail)


def recurrent_backward(
    place, pieces, local_grad, after_keep, mixed_grad, branch, states, carry_in, pre, conv_low,
    dist, inputs, halo, conv_weight, decay, gate_weights,
):
    rows, width = branch.shape
    shards = pieces.shape[0]
    tile = 256
    tiles_n = rows // tile
    blocks = tile // 8

    def body(
        place_ref, pieces_ref, lg_ref, ak_ref, mg_ref, branch_ref, states_ref, before_ref, carry_ref,
        pre_ref, conv_ref, dist_ref, in_ref, in_before_ref, halo_ref, cw_ref, dp_ref, gw_ref,
        bl_ref, il_ref, pl_ref, sums_ref, end_ref, edge_ref,
        back, prev, ext, acc, cg,
    ):
        i = pl.program_id(0)
        mine = place_ref[0]

        @pl.when(i == 0)
        def _():
            entering = jnp.zeros((1, width), F32)
            for s in range(shards - 1, 0, -1):
                longer = pieces_ref[s, 0:1] * entering + pieces_ref[s, 1:2]
                entering = jnp.where(s > mine, longer, entering)
            back[...] = jnp.broadcast_to(entering, (8, width))
            sums_ref[...] = jnp.zeros_like(sums_ref)
            acc[tile : tile + 16] = jnp.zeros((16, width), F32)

        @pl.when(i > 0)
        def _():
            acc[tile : tile + 8] = acc[0:8]
            acc[tile + 8 : tile + 16] = jnp.zeros((8, width), F32)

        @pl.when(i == tiles_n - 1)
        def _():
            prev[0:8] = carry_ref[...]
            ext[0:8] = halo_ref[...]

        @pl.when(i < tiles_n - 1)
        def _():
            prev[0:8] = before_ref[...]
            ext[0:8] = in_before_ref[...]

        prev[8 : 8 + tile] = states_ref[...]
        ext[8 : 8 + tile] = in_ref[...]
        acc[0:tile] = jnp.zeros((tile, width), F32)
        dist = dist_ref[...]
        notstart = dist > 0
        for lane in range(0, width, LANES):
            cut = slice(lane, lane + LANES)
            far = slice(width + lane, width + lane + LANES)
            grad = lg_ref[:, cut] + ak_ref[:, cut] * back[0:1, cut]
            _, slope = gelu_both(branch_ref[:, cut])
            bl_ref[:, cut] = (mg_ref[:, cut].astype(F32) * states_ref[:, cut] * slope).astype(BF16)
            reset = sigmoid(pre_ref[:, cut])
            gate = sigmoid(pre_ref[:, far])
            power = -GATE_POWER * softplus_neg(dp_ref[:, cut])
            keep = jnp.exp(power * reset)
            inside = 1.0 - keep * keep + ROOT_FLOOR
            unroot = lax.rsqrt(inside)
            root = inside * unroot
            conv = conv_ref[:, cut].astype(F32)
            through = gate * conv
            keep_grad = jnp.where(notstart, grad * prev[7 : 7 + tile, cut], 0.0) - grad * through * (
                keep * unroot
            )
            kg = keep_grad * keep * reset
            pl_ref[:, cut] = (kg * power * (1.0 - reset)).astype(BF16)
            rooted = grad * root
            cg[:, cut] = rooted * gate
            pl_ref[:, far] = (rooted * through * (1.0 - gate)).astype(BF16)
            sums_ref[40:48, cut] += jnp.sum(kg.reshape(blocks, 8, LANES), axis=0)
        cg[...] += mm(pl_ref[...], gw_ref[...], NT)
        for lane in range(0, width, LANES):
            cut = slice(lane, lane + LANES)
            conv_grad = cg[:, cut]
            sums_ref[32:40, cut] += jnp.sum(conv_grad.reshape(blocks, 8, LANES), axis=0)
            for k in range(CONV):
                masked = conv_grad if k == 0 else jnp.where(dist >= k, conv_grad, 0.0)
                tap = masked * ext[8 - k : 8 - k + tile, cut]
                sums_ref[8 * k : 8 * k + 8, cut] += jnp.sum(tap.reshape(blocks, 8, LANES), axis=0)
                acc[8 - k : 8 - k + tile, cut] += cw_ref[k : k + 1, cut] * masked
        il_ref[...] = acc[8 : 8 + tile].astype(BF16)

        @pl.when(i == 0)
        def _():
            end_ref[...] = acc[tile : tile + 8]

        @pl.when(i == tiles_n - 1)
        def _():
            edge_ref[...] = acc[0:8]

    tiles = pl.BlockSpec((tile, width), lambda i, *_: (tiles_n - 1 - i, 0))
    wide = pl.BlockSpec((tile, 2 * width), lambda i, *_: (tiles_n - 1 - i, 0))
    before = pl.BlockSpec(
        (8, width), lambda i, *_: (jnp.maximum((tiles_n - 1 - i) * blocks - 1, 0), 0)
    )
    small = whole((8, width))
    return call(
        body,
        (tiles_n,),
        [
            whole(pieces.shape), tiles, tiles, tiles, tiles, tiles, before, small, wide, tiles,
            pl.BlockSpec((tile, 1), lambda i, *_: (tiles_n - 1 - i, 0)),
            tiles, before, small, whole((CONV, width)), whole((1, width)), whole((width, 2 * width)),
        ],
        [tiles, tiles, wide, whole((48, width)), small, small],
        [
            struct((rows, width), BF16),
            struct((rows, width), BF16),
            struct((rows, 2 * width), BF16),
            struct((48, width), F32),
            struct((8, width), F32),
            struct((8, width), F32),
        ],
        [
            pltpu.VMEM((8, width), F32),
            pltpu.VMEM((tile + 8, width), F32),
            pltpu.VMEM((tile + 8, width), F32),
            pltpu.VMEM((tile + 16, width), F32),
            pltpu.VMEM((tile, width), F32),
        ],
        prefetch=1,
        flops=4 * rows * width * width + 300 * rows * width,
        moved=40 * rows * width,
    )(
        place, pieces, local_grad, after_keep, mixed_grad, branch, states, states, carry_in, pre,
        conv_low, dist, inputs, inputs, halo, conv_weight, decay, gate_weights,
    )


def input_backward(place, branch_low, inputs_low, end, returned, weights, stream, gain, resid_grads):
    rows, width = branch_low.shape
    model = stream.shape[1]
    sub = resid_grads[0].shape[0]
    tile = sub * CHUNKS
    steps = rows // tile

    def body(
        place_ref, bl_ref, il_ref, end_ref, ret_ref, w_ref, x_ref, gain_ref, *rest
    ):
        part_ref, fixed_ref, sum_ref = rest[CHUNKS:]
        i = pl.program_id(0)
        fixed_ref[...] = il_ref[...]

        @pl.when(i == steps - 1)
        def _():
            tail = jnp.concatenate(
                [il_ref[tile - 16 : tile - 8].astype(F32), end_ref[...] + ret_ref[...]], axis=0
            )
            fixed_ref[tile - 16 : tile] = tail.astype(BF16)

        g = mm(bl_ref[...], w_ref[:, :width], NT) + mm(fixed_ref[...], w_ref[:, width:], NT)
        x = x_ref[...].astype(F32)
        inv = lax.rsqrt(jnp.mean(x * x, axis=-1, keepdims=True) + EPSILON)
        unit = x * inv
        scaled = g * gain_ref[...]
        dot = jnp.mean(scaled * unit, axis=-1, keepdims=True)
        part = inv * (scaled - unit * dot)
        sums = jnp.sum(g * unit, axis=0, keepdims=True)

        @pl.when(i == 0)
        def _():
            sum_ref[...] = sums

        @pl.when(i > 0)
        def _():
            sum_ref[...] += sums

        @pl.when(i == place_ref[1])
        def _():
            for c in range(CHUNKS):
                cut = slice(c * sub, (c + 1) * sub)
                part_ref[cut] = (part[cut] + rest[c][...]).astype(BF16)

        @pl.when(i != place_ref[1])
        def _():
            part_ref[...] = part.astype(BF16)

    tiles = pl.BlockSpec((tile, width), lambda i, *_: (i, 0))
    wide = pl.BlockSpec((tile, model), lambda i, *_: (i, 0))
    return call(
        body,
        (steps,),
        [
            tiles, tiles, whole((8, width)), whole((8, width)), whole((model, 2 * width)), wide,
            whole((1, model)),
        ]
        + [whole((sub, model))] * CHUNKS,
        [wide, tiles, whole((1, model))],
        [struct((rows, model), BF16), struct((rows, width), BF16), struct((1, model), F32)],
        prefetch=1,
        flops=4 * rows * width * model + 30 * rows * model,
        moved=4 * rows * model + 4 * width * model + 6 * rows * width,
    )(place, branch_low, inputs_low, end, returned, weights, stream, gain, *resid_grads)


def block_diagonal(blocks, width):
    heads, size = blocks.shape[0], blocks.shape[1]
    rows = [
        jnp.pad(blocks[h], ((0, 0), (h * size, width - (h + 1) * size))) for h in range(heads)
    ]
    return jnp.pad(jnp.concatenate(rows, axis=0), ((0, width - heads * size), (0, 0)))


def diagonal_blocks(full, heads, size):
    return jnp.stack([full[h * size : (h + 1) * size, h * size : (h + 1) * size] for h in range(heads)])


def shards(
    tokens,
    cotangent,
    destination,
    lengths,
    norm_gain,
    w_branch,
    w_input,
    conv_weight,
    conv_bias,
    w_recur,
    w_ingate,
    decay_param,
    w_out,
    mlp_gain,
    w_gate,
    w_up,
    w_down,
):
    shard_count = lax.axis_size("seq")
    my_shard = lax.axis_index("seq")
    model_count = lax.axis_size("mp")
    my_model = lax.axis_index("mp")
    row_count, model_width = tokens.shape
    slab_width = model_width // model_count
    per_peer = row_count // shard_count
    own_rows = row_count // model_count
    sub = own_rows // CHUNKS
    channels = w_branch.shape[1]
    heads, block_width = w_recur.shape[0], w_recur.shape[1]
    width = -(-channels // LANES) * LANES
    parity = my_shard % 2
    place = jnp.stack([my_shard, my_model, parity]).astype(jnp.int32)
    pad_lanes = functools.partial(jnp.pad, pad_width=((0, 0), (0, width - channels)))

    bits = shard_count.bit_length() - 1

    def scatter_sum(x, axis, dim):
        return lax.psum_scatter(x, axis, scatter_dimension=dim, tiled=True)

    def exchange(x, axis):
        return lax.all_to_all(x, axis, split_axis=0, concat_axis=0, tiled=True)

    def swap(x, bit):
        return lax.ppermute(x, "seq", [(i, i ^ (1 << bit)) for i in range(shard_count)])

    def add_low(left, right):
        return (left.astype(F32) + right.astype(F32)).astype(BF16)

    def tie(*values):
        return lax.optimization_barrier(values)

    def tie_with(value, ring, running):
        value, ring, arrays = tie(value, ring, [x for x, _ in running])
        return value, ring, [(x, up) for x, (_, up) in zip(arrays, running)]

    def halve_once(x, up, bits):
        done = bits - x.shape[0].bit_length() + 1
        bit = done if up else bits - done
        mine = (my_shard >> bit) & 1
        axis = 1 if up else 0
        x = x.reshape(-1, 2, *x.shape[1:]) if up else x.reshape(2, -1, *x.shape[1:])
        other = lax.dynamic_index_in_dim(x, 1 - mine, axis, False)
        return add_low(lax.dynamic_index_in_dim(x, mine, axis, False), swap(other, bit))

    def ring_start(x):
        return ((x, x), (x,), ())

    def ring_step(ring):
        (right, left), rights, lefts = ring
        right = lax.ppermute(right, "mp", [(i, i + 1) for i in range(model_count - 1)])
        left = lax.ppermute(left, "mp", [(i + 1, i) for i in range(model_count - 1)])
        return ((right, left), rights + (right,), lefts + (left,))

    def ring_end(ring):
        _, rights, lefts = ring
        return [rights[0]] + [
            jnp.where(my_model >= k, rights[k], lefts[model_count - k - 1])
            for k in range(1, model_count)
        ]

    local_dest = lax.dynamic_slice_in_dim(destination, my_shard * row_count, row_count)
    dest_row, dest_col = local_dest.reshape(1, -1), local_dest.reshape(-1, 1)
    straight = jnp.zeros((1,), jnp.int32)
    turn = (my_shard * per_peer).astype(jnp.int32)[None]
    arrived_tokens = exchange(send_order(straight, dest_row, dest_col, tokens), "seq")
    sent_cot = send_order(turn, dest_row, dest_col, cotangent)
    sorted_dest = jnp.sort(destination.reshape(shard_count, row_count), axis=1)
    landing = (
        lax.dynamic_slice_in_dim(sorted_dest, my_shard * per_peer, per_peer, 1).reshape(-1)
        - my_shard * row_count
    )
    landing_row = landing.reshape(1, -1)
    turned = jnp.stack(
        [
            lax.dynamic_index_in_dim(landing.reshape(shard_count, per_peer), my_shard ^ k, 0, False)
            for k in range(shard_count)
        ]
    ).reshape(1, -1)
    mlp_place = np.arange(row_count, dtype=np.int32).reshape(model_count, CHUNKS, sub)
    mlp_place = jnp.asarray(mlp_place.transpose(1, 0, 2).reshape(-1, 1))
    mlp_landing = (
        (landing % own_rows) // sub * (model_count * sub) + landing // own_rows * sub + landing % sub
    )

    positions = my_shard * row_count + jnp.arange(row_count, dtype=jnp.int32)
    count = lengths.shape[0]
    earlier = np.tril(np.ones((count, count), np.int32), -1)
    seq_starts = jnp.sum(jnp.asarray(earlier) * lengths[None, :], axis=1)
    seq_start = jnp.max(
        jnp.where(seq_starts[None, :] <= positions[:, None], seq_starts[None, :], 0), axis=1
    )
    dist = (positions - seq_start).reshape(-1, 1)

    w_rec = jnp.concatenate([pad_lanes(w_branch), pad_lanes(w_input)], axis=1)
    w_gates = jnp.concatenate(
        [block_diagonal(w_recur, width), block_diagonal(w_ingate, width)], axis=1
    )
    taps = pad_lanes(conv_weight)
    bias = pad_lanes(conv_bias[None])
    decay = pad_lanes(decay_param[None])
    gain = norm_gain[None]
    gain2 = mlp_gain[None]
    half = model_width // 2
    w_out_half = jnp.pad(
        lax.dynamic_slice_in_dim(w_out, parity * half, half, 1), ((0, width - channels), (0, 0))
    )
    w_near = lax.all_gather(w_out_half, "mp", axis=0)

    arrived_tokens, sent_cot, w_rec, w_gates = lax.optimization_barrier(
        (arrived_tokens, sent_cot, w_rec, w_gates)
    )
    stream, hidden_near, hidden_far, branch, inputs = project(
        place, landing_row, arrived_tokens, gain, w_rec, shard_count
    )
    halo = lax.ppermute(
        inputs[row_count - 8 :], "seq", [(i, i + 1) for i in range(shard_count - 1)]
    )
    conv_low, pre, keep, prefix, local, tail = recurrent_forward(
        inputs, halo, dist, taps, bias, decay, w_gates
    )
    pieces = lax.all_gather(tail, "seq")
    pieces, sent_cot, w_near = tie(pieces, sent_cot, w_near)
    cot_blocks = [sent_cot[:per_peer]]
    for k in range(1, shard_count):
        block = sent_cot[k * per_peer : (k + 1) * per_peer]
        cot_blocks.append(
            lax.ppermute(block, "seq", [(i, i ^ k) for i in range(shard_count)])
        )
    w_far = swap(w_near, 0)
    states, mixed, carry_in = finish_states(place, pieces, local, prefix, branch, model_count)

    resids, normeds = [], []
    upstream, upstream_near, upstream_far = place_upstream(
        place, mlp_place, turned, cot_blocks, shard_count
    )
    for c in range(CHUNKS):
        mixed_full = exchange(mixed[c], "mp")
        if c == CHUNKS - 1:
            mixed_full, upstream = tie(mixed_full, upstream)
        resid_own, normed_own = output_rows(c, place, mixed_full, w_near, w_far, stream, gain2)
        resids.append(resid_own)
        normeds.append(normed_own)
    kept, grads = (), []
    for c in range(CHUNKS):
        normed = lax.all_gather(normeds[c], "mp", axis=0, tiled=True)
        *kept, grad = mlp_chunk(
            c, place, normed, upstream, resids[c], w_gate, w_up, w_down, shard_count, kept
        )
        grads.append(scatter_sum(grad, "mp", 0))
    inner_act, gate_low, up_low, normed_near, normed_far, block_part = kept

    parts = shard_count // 2
    part_width = model_width // shard_count
    hidden_units = w_gate.shape[1]

    def outer(left, right):
        return mm(left, right, TN).astype(BF16)

    def with_partner(near, sent, right):
        return (mm(near, right, TN) + sent.astype(F32)).astype(BF16).reshape(
            parts, part_width, right.shape[1]
        )

    far_gate = outer(normed_far, gate_low)
    far_up = outer(normed_far, up_low)
    far_down = outer(upstream_far, inner_act)
    grads[0], far_gate, far_up, far_down = tie(grads[0], far_gate, far_up, far_down)
    far_gate, far_up, far_down = swap(far_gate, 0), swap(far_up, 0), swap(far_down, 0)
    resid_grads, resid_lows, mixed_grads, mlp_gain_part = [], [], [], 0.0
    for c in range(CHUNKS):
        resid_grad, resid_low, mixed_grad_full, gain_part = resid_backward(
            c, place, grads[c], upstream, resids[c], gain2, w_near, w_far
        )
        if c == 0:
            mixed_grad_full, gate_low, up_low, inner_act = tie(
                mixed_grad_full, gate_low, up_low, inner_act
            )
            grad_gate = with_partner(normed_near, far_gate, gate_low)
            grad_up = with_partner(normed_near, far_up, up_low)
            grad_down = with_partner(upstream_near, far_down, inner_act)
            grads[1], grad_gate, grad_up, grad_down = tie(grads[1], grad_gate, grad_up, grad_down)
        mlp_gain_part = mlp_gain_part + gain_part
        resid_grads.append(resid_grad)
        resid_lows.append(resid_low)
        mixed_grads.append(exchange(mixed_grad_full, "mp"))
    halves = (grad_down[..., : hidden_units // 2], grad_down[..., hidden_units // 2 :])
    running = [
        (grad_gate, True),
        (grad_up, False),
        (halves[0], True),
        (halves[1], False),
    ]

    def step(entries):
        return [(halve_once(x, up, bits), up) for x, up in entries]

    mixed_grads[-1], *resid_lows = tie(mixed_grads[-1], *resid_lows)
    ring = ring_start(jnp.stack(resid_lows))
    block_share = scatter_sum(block_part, "mp", 1)
    local_grad, after_keep, edge_pair, mixed_grad = recurrent_back_scan(
        mixed_grads, branch, keep, tail
    )
    back_pieces = lax.all_gather(edge_pair, "seq")
    branch_low, inputs_part, pre_low, sums, end, edge = recurrent_backward(
        place, back_pieces, local_grad, after_keep, mixed_grad, branch, states, carry_in, pre,
        conv_low, dist, inputs, halo, taps, decay, w_gates,
    )
    returned = lax.ppermute(edge, "seq", [(i + 1, i) for i in range(shard_count - 1)])
    running = step(running)
    ring = ring_step(ring)
    returned, ring, running = tie_with(returned, ring, running)
    returned, block_share = tie(returned, block_share)
    input_part, inputs_low, norm_gain_part = input_backward(
        place, branch_low, inputs_part, end, returned, w_rec, stream, gain, resid_grads
    )
    ring = ring_step(ring)
    input_part, ring, running = tie_with(input_part, ring, running)
    for _ in range(bits - 2):
        running = step(running)
    for _ in range(model_count - 3):
        ring = ring_step(ring)
    input_share = scatter_sum(input_part, "mp", 1)
    sent_gate, sent_up, *sent_down = [x[0] for x, _ in running]
    sent_gate, sent_up = sent_gate.astype(F32), sent_up.astype(F32)
    sent_down = jnp.concatenate(sent_down, axis=-1).astype(F32).T

    gathered = ring_end(ring)
    mixed_near = [
        lax.dynamic_index_in_dim(mixed, (my_model - k) % model_count, 1, False)
        for k in range(model_count)
    ]
    grad_out = mm(
        jnp.stack(mixed_near).reshape(row_count, width),
        jnp.stack(gathered).reshape(row_count, model_width),
        TN,
    ).astype(BF16)
    sent_out = scatter_sum(grad_out, "seq", 1)
    grad_gates = mm(conv_low, pre_low, TN)
    rec_low = jnp.concatenate([branch_low, inputs_low], axis=1)
    grad_rec = with_partner(hidden_near, swap(outer(hidden_far, rec_low), 0), rec_low)
    running = [(grad_rec[..., :width], True), (grad_rec[..., width:], False)]
    for _ in range(bits - 1):
        running = step(running)
    sent_branch, sent_input = [x[0] for x, _ in running]
    sent_branch = sent_branch[:, :channels].astype(F32)
    sent_input = sent_input[:, :channels].astype(F32)
    all_rows = jnp.arange(row_count, dtype=jnp.int32)[None]
    home_block = exchange(place_rows(mlp_landing.reshape(-1, 1), all_rows, block_share), "seq")
    input_share, sent_branch, sent_input, home_block, sent_gate, sent_up, sent_down = tie(
        input_share, sent_branch, sent_input, home_block, sent_gate, sent_up, sent_down
    )

    sums = jnp.sum(sums.reshape(CONV + 2, 8, width), axis=1)[:, :channels]
    sums = jnp.concatenate(
        [sums[: CONV + 1], sums[CONV + 1 :] * (GATE_POWER * jax.nn.sigmoid(-decay_param))], axis=0
    )
    gains = jnp.concatenate([norm_gain_part, mlp_gain_part], axis=0)
    gains = gains.reshape(2, model_count, slab_width).transpose(1, 0, 2)
    gains = jnp.sum(exchange(gains, "mp"), axis=0)
    sum_rows = sums.size // block_width
    gain_rows = -(-gains.size // block_width)
    gains = jnp.pad(gains.reshape(-1), (0, gain_rows * block_width - gains.size))
    extra = jnp.concatenate(
        [sums.reshape(sum_rows, block_width), gains.reshape(gain_rows, block_width)], axis=0
    )
    extra = jnp.pad(extra, ((0, block_width - sum_rows - gain_rows), (0, 0)))
    small = jnp.concatenate(
        [
            diagonal_blocks(grad_gates[:, :width], heads, block_width),
            diagonal_blocks(grad_gates[:, width:], heads, block_width),
            extra[None],
        ],
        axis=0,
    )
    small = lax.psum(small, "seq")
    input_share, small, sent_out = tie(input_share, small, sent_out)
    sent_out = sent_out[:channels].astype(F32)
    sums = small[2 * heads, :sum_rows].reshape(CONV + 2, channels)
    gains = small[2 * heads, sum_rows : sum_rows + gain_rows].reshape(-1)
    gains = gains[: 2 * slab_width].reshape(2, slab_width)

    home_input = exchange(place_rows(landing.reshape(-1, 1), all_rows, input_share), "seq")
    block_out = restore_rows(dest_row, dest_col, home_block)
    input_grad = restore_rows(dest_row, dest_col, home_input)
    return (
        block_out,
        input_grad,
        gains[0],
        sent_branch,
        sent_input,
        sums[:CONV],
        sums[CONV],
        small[:heads],
        small[heads : 2 * heads],
        sums[CONV + 1],
        sent_out,
        gains[1],
        sent_gate,
        sent_up,
        sent_down,
    )


def solution(mesh):
    in_specs = (
        P("seq", None),
        P("seq", None),
        P(),
        P(),
        P(),
        P(None, "mp"),
        P(None, "mp"),
        P(None, "mp"),
        P("mp"),
        P("mp", None, None),
        P("mp", None, None),
        P("mp"),
        P("mp", None),
        P(),
        P(None, "mp"),
        P(None, "mp"),
        P("mp", None),
    )
    out_specs = (
        P("seq", "mp"),
        P("seq", "mp"),
        P("mp"),
        P("seq", "mp"),
        P("seq", "mp"),
        P(None, "mp"),
        P("mp"),
        P("mp", None, None),
        P("mp", None, None),
        P("mp"),
        P("mp", "seq"),
        P("mp"),
        P("seq", "mp"),
        P("seq", "mp"),
        P("mp", "seq"),
    )
    return jax.shard_map(shards, mesh=mesh, in_specs=in_specs, out_specs=out_specs, check_vma=False)
```

```python
import functools

import jax
import jax.numpy as jnp
import numpy as np
from jax import lax
from jax.experimental import pallas as pl
from jax.experimental.pallas import tpu as pltpu
from jax.sharding import PartitionSpec as P

CONV = 4
EPSILON = 1e-06
GATE_POWER = 8.0
ROOT_FLOOR = 0.01
LANES = 128
GROUP = 8
CHUNKS = 2
F32 = jnp.float32
BF16 = jnp.bfloat16
MIB = 1 << 20
GELU_A = 0.7978845608028654
GELU_B = 0.044715

NN = (((1,), (0,)), ((), ()))
NT = (((1,), (1,)), ((), ()))
TN = (((0,), (0,)), ((), ()))


def mm(left, right, dims=NN):
    return lax.dot_general(left, right, dims, preferred_element_type=F32)


def call(body, grid, in_specs, out_specs, out_shape, scratch=(), prefetch=0, aliases=None, flops=0, moved=0):
    return pl.pallas_call(
        body,
        grid_spec=pltpu.PrefetchScalarGridSpec(
            num_scalar_prefetch=prefetch,
            grid=grid,
            in_specs=in_specs,
            out_specs=out_specs,
            scratch_shapes=list(scratch),
        ),
        out_shape=out_shape,
        input_output_aliases=aliases or {},
        compiler_params=pltpu.CompilerParams(
            dimension_semantics=("arbitrary",) * len(grid), vmem_limit_bytes=60 * MIB
        ),
        cost_estimate=pl.CostEstimate(
            flops=flops, bytes_accessed=moved, transcendentals=0
        ),
    )


def whole(shape):
    zeros = (0,) * len(shape)
    return pl.BlockSpec(shape, lambda *_: zeros)


def struct(shape, dtype):
    return jax.ShapeDtypeStruct(shape, dtype)


def sigmoid(x):
    return 0.5 * jnp.tanh(0.5 * x) + 0.5


def gelu(x):
    return 0.5 * x * (1.0 + jnp.tanh(GELU_A * (x + GELU_B * x * x * x)))


def gelu_both(x):
    square = x * x
    t = jnp.tanh(GELU_A * x * (1.0 + GELU_B * square))
    half = 0.5 * (1.0 + t)
    slope = half + 0.5 * x * (1.0 - t * t) * (GELU_A * (1.0 + 3.0 * GELU_B * square))
    return x * half, slope


def softplus_neg(x):
    return jnp.log1p(jnp.exp(-jnp.abs(x))) + jnp.maximum(-x, 0.0)


def one_hot(rows, lanes):
    return jnp.where(rows == lanes, 1.0, 0.0).astype(BF16)


def send_order(turn, dest_row, dest_col, values):
    rows, width = values.shape
    tile = 256

    def body(turn_ref, row_ref, col_ref, val_ref, out_ref, rank_ref):
        i = pl.program_id(0)

        @pl.when(i == 0)
        def _():
            before = jnp.where(col_ref[...] < row_ref[...], 1.0, 0.0)
            rank = jnp.sum(before, axis=0, keepdims=True).astype(jnp.int32)
            rank_ref[...] = rank ^ turn_ref[0]

        place = lax.broadcasted_iota(jnp.int32, (tile, rows), 0) + i * tile
        out_ref[...] = mm(one_hot(place, rank_ref[...]), val_ref[...]).astype(BF16)

    return call(
        body,
        (rows // tile,),
        [whole((1, rows)), whole((rows, 1)), whole((rows, width))],
        pl.BlockSpec((tile, width), lambda i, *_: (i, 0)),
        struct((rows, width), BF16),
        [pltpu.VMEM((1, rows), jnp.int32)],
        prefetch=1,
        flops=2 * rows * rows * width,
        moved=4 * rows * width,
    )(turn, dest_row, dest_col, values)


def send_blocks(turn, dest_row, dest_col, values, count):
    rows, width = values.shape
    size = rows // count

    def body(turn_ref, row_ref, col_ref, val_ref, *refs):
        rank_ref = refs[count]
        i = pl.program_id(0)

        @pl.when(i == 0)
        def _():
            before = jnp.where(col_ref[...] < row_ref[...], 1.0, 0.0)
            rank = jnp.sum(before, axis=0, keepdims=True).astype(jnp.int32)
            rank_ref[...] = rank ^ turn_ref[0]

        spot = lax.broadcasted_iota(jnp.int32, (size, rows), 0) + i * size
        moved = mm(one_hot(spot, rank_ref[...]), val_ref[...]).astype(BF16)
        for k in range(count):

            @pl.when(i == k)
            def _(k=k):
                refs[k][...] = moved

    return call(
        body,
        (count,),
        [whole((1, rows)), whole((rows, 1)), whole((rows, width))],
        [whole((size, width))] * count,
        [struct((size, width), BF16)] * count,
        [pltpu.VMEM((1, rows), jnp.int32)],
        prefetch=1,
        flops=2 * rows * rows * width,
        moved=4 * rows * width,
    )(turn, dest_row, dest_col, values)


def place_rows(place_col, landing_row, values):
    rows, width = values.shape
    tile = 256

    def body(place_ref, land_ref, val_ref, out_ref):
        out_ref[...] = mm(one_hot(place_ref[...], land_ref[...]), val_ref[...]).astype(out_ref.dtype)

    return call(
        body,
        (rows // tile,),
        [pl.BlockSpec((tile, 1), lambda i: (i, 0)), whole((1, rows)), whole((rows, width))],
        pl.BlockSpec((tile, width), lambda i: (i, 0)),
        struct((rows, width), BF16),
        flops=2 * rows * rows * width,
        moved=4 * rows * width,
    )(place_col, landing_row, values)


def split_columns(near_ref, far_ref, values, parity, parts):
    size = values.shape[1] // parts
    for q in range(parts // 2):
        to = slice(q * size, (q + 1) * size)
        even = values[:, 2 * q * size : (2 * q + 1) * size]
        odd = values[:, (2 * q + 1) * size : (2 * q + 2) * size]
        near_ref[:, to] = jnp.where(parity == 0, even, odd)
        far_ref[:, to] = jnp.where(parity == 0, odd, even)


def place_upstream(place, place_col, landing_row, blocks, parts):
    count = len(blocks)
    size, width = blocks[0].shape
    rows = count * size
    tile = 256

    def body(my_ref, place_ref, land_ref, *refs):
        out_ref, near_ref, far_ref, val_ref, sem = refs[count:]

        @pl.when(pl.program_id(0) == 0)
        def _():
            copies = [
                pltpu.make_async_copy(refs[k], val_ref.at[k * size : (k + 1) * size], sem.at[k])
                for k in range(count)
            ]
            for copy in copies:
                copy.start()
            for copy in copies:
                copy.wait()

        moved = mm(one_hot(place_ref[...], land_ref[...]), val_ref[...]).astype(BF16)
        out_ref[...] = moved
        split_columns(near_ref, far_ref, moved, my_ref[2], parts)

    return call(
        body,
        (rows // tile,),
        [pl.BlockSpec((tile, 1), lambda i, *_: (i, 0)), whole((1, rows))]
        + [pl.BlockSpec(memory_space=pl.ANY)] * count,
        [
            pl.BlockSpec((tile, width), lambda i, *_: (i, 0)),
            pl.BlockSpec((tile, width // 2), lambda i, *_: (i, 0)),
            pl.BlockSpec((tile, width // 2), lambda i, *_: (i, 0)),
        ],
        [
            struct((rows, width), BF16),
            struct((rows, width // 2), BF16),
            struct((rows, width // 2), BF16),
        ],
        [pltpu.VMEM((rows, width), BF16), pltpu.SemaphoreType.DMA((count,))],
        prefetch=1,
        flops=2 * rows * rows * width,
        moved=6 * rows * width,
    )(place, place_col, landing_row, *blocks)


def restore_rows(dest_row, dest_col, values):
    rows, width = values.shape
    tile = 256

    def body(row_ref, col_ref, val_ref, out_ref):
        before = jnp.where(row_ref[...] < col_ref[...], 1.0, 0.0)
        rank = jnp.sum(before, axis=1, keepdims=True).astype(jnp.int32)
        spot = lax.broadcasted_iota(jnp.int32, (tile, rows), 1)
        out_ref[...] = mm(one_hot(spot, rank), val_ref[...])

    return call(
        body,
        (rows // tile,),
        [whole((1, rows)), pl.BlockSpec((tile, 1), lambda i: (i, 0)), whole((rows, width))],
        pl.BlockSpec((tile, width), lambda i: (i, 0)),
        struct((rows, width), F32),
        flops=2 * rows * rows * width,
        moved=6 * rows * width,
    )(dest_row, dest_col, values)


def project(place, landing_row, arrived, gain, w_branch, w_input, half, parts):
    rows, width = arrived.shape
    channels = w_branch.shape[0]
    wide = 2 * half
    tile = 256

    def body(
        my_ref, land_ref, arr_ref, gain_ref, wb_ref, wi_ref, stream_ref, near_ref, far_ref, branch_ref, inputs_ref
    ):
        i = pl.program_id(0)
        place = lax.broadcasted_iota(jnp.int32, (tile, rows), 0) + i * tile
        x = mm(one_hot(place, land_ref[...]), arr_ref[...])
        stream_ref[...] = x.astype(BF16)
        inv = lax.rsqrt(jnp.mean(x * x, axis=-1, keepdims=True) + EPSILON)
        hidden = (x * inv * gain_ref[...]).astype(BF16)
        split_columns(near_ref, far_ref, hidden, my_ref[2], parts)
        for out_ref, w_ref in ((branch_ref, wb_ref), (inputs_ref, wi_ref)):
            if channels < half:
                out_ref[...] = jnp.zeros_like(out_ref)
            out_ref[:, :channels] = mm(hidden, w_ref[...], NT)

    return call(
        body,
        (rows // tile,),
        [whole((1, rows)), whole((rows, width)), whole((1, width))] + [whole((channels, width))] * 2,
        [
            pl.BlockSpec((tile, width), lambda i, *_: (i, 0)),
            pl.BlockSpec((tile, width // 2), lambda i, *_: (i, 0)),
            pl.BlockSpec((tile, width // 2), lambda i, *_: (i, 0)),
            pl.BlockSpec((tile, half), lambda i, *_: (i, 0)),
            pl.BlockSpec((tile, half), lambda i, *_: (i, 0)),
        ],
        [
            struct((rows, width), BF16),
            struct((rows, width // 2), BF16),
            struct((rows, width // 2), BF16),
            struct((rows, half), F32),
            struct((rows, half), F32),
        ],
        prefetch=1,
        flops=2 * rows * width * (rows + wide),
        moved=6 * rows * width + 2 * width * wide + 4 * rows * wide,
    )(place, landing_row, arrived, gain, w_branch, w_input)


def tile_scan(rates, drives, keep_in, state_in, reverse):
    rows, lanes = rates.shape
    groups = rows // GROUP
    a = rates.reshape(groups, GROUP, lanes)
    d = drives.reshape(groups, GROUP, lanes)
    spot = lax.broadcasted_iota(jnp.int32, (groups, GROUP, lanes), 1)
    for by in (1, 2, 4):
        turn = GROUP - by if reverse else by
        ok = spot < GROUP - by if reverse else spot >= by
        d_near = pltpu.roll(d, turn, 1)
        a_near = pltpu.roll(a, turn, 1)
        d = jnp.where(ok, a * d_near + d, d)
        a = jnp.where(ok, a * a_near, a)
    end = 0 if reverse else GROUP - 1
    keeps, states = [None] * groups, [None] * groups
    for g in range(groups - 1, -1, -1) if reverse else range(groups):
        keeps[g] = a[g] * keep_in
        states[g] = d[g] + a[g] * state_in
        keep_in = keeps[g][end : end + 1]
        state_in = states[g][end : end + 1]
    return jnp.concatenate(keeps, 0), jnp.concatenate(states, 0), keep_in, state_in


def recurrent_forward(inputs, halo, dist, conv_weight, conv_bias, decay, gate_weights):
    rows, width = inputs.shape
    tile = 256
    last = rows // tile - 1

    def body(
        in_ref, halo_ref, dist_ref, cw_ref, cb_ref, dp_ref, gw_ref,
        conv_ref, pre_ref, keep_ref, prefix_ref, local_ref, tail_ref,
        ext, carry,
    ):
        i = pl.program_id(0)

        @pl.when(i == 0)
        def _():
            ext[0:8] = halo_ref[...]
            carry[0:1] = jnp.ones((1, width), F32)
            carry[1:2] = jnp.zeros((1, width), F32)

        @pl.when(i > 0)
        def _():
            ext[0:8] = ext[tile : tile + 8]

        ext[8 : 8 + tile] = in_ref[...]
        dist = dist_ref[...]
        conv = cb_ref[...] + cw_ref[0:1] * ext[8 : 8 + tile]
        for k in range(1, CONV):
            conv = conv + jnp.where(dist >= k, cw_ref[k : k + 1] * ext[8 - k : 8 - k + tile], 0.0)
        conv_low = conv.astype(BF16)
        conv_ref[...] = conv_low
        pre_ref[...] = mm(conv_low, gw_ref[...])
        notstart = dist > 0
        for lane in range(0, width, LANES):
            cut = slice(lane, lane + LANES)
            far = slice(width + lane, width + lane + LANES)
            reset = sigmoid(pre_ref[:, cut])
            gate = sigmoid(pre_ref[:, far])
            keep = jnp.exp((-GATE_POWER * softplus_neg(dp_ref[:, cut])) * reset)
            drive = jnp.sqrt(1.0 - keep * keep + ROOT_FLOOR) * (gate * conv_ref[:, cut].astype(F32))
            rate = jnp.where(notstart, keep, 0.0)
            keep_ref[:, cut] = rate
            keeps, states, keep_out, state_out = tile_scan(
                rate, drive, carry[0:1, cut], carry[1:2, cut], False
            )
            prefix_ref[:, cut] = keeps
            local_ref[:, cut] = states
            carry[0:1, cut] = keep_out
            carry[1:2, cut] = state_out

        @pl.when(i == last)
        def _():
            tail_ref[...] = carry[...]

    tiles = pl.BlockSpec((tile, width), lambda i: (i, 0))
    return call(
        body,
        (rows // tile,),
        [
            tiles,
            whole((8, width)),
            pl.BlockSpec((tile, 1), lambda i: (i, 0)),
            whole((CONV, width)),
            whole((1, width)),
            whole((1, width)),
            whole((width, 2 * width)),
        ],
        [
            tiles,
            pl.BlockSpec((tile, 2 * width), lambda i: (i, 0)),
            tiles,
            tiles,
            tiles,
            whole((8, width)),
        ],
        [
            struct((rows, width), BF16),
            struct((rows, 2 * width), F32),
            struct((rows, width), F32),
            struct((rows, width), F32),
            struct((rows, width), F32),
            struct((8, width), F32),
        ],
        [pltpu.VMEM((tile + 8, width), F32), pltpu.VMEM((8, width), F32)],
        flops=4 * rows * width * width + 200 * rows * width,
        moved=30 * rows * width,
    )(inputs, halo, dist, conv_weight, conv_bias, decay, gate_weights)


def finish_states(place, pieces, local, prefix, branch, owners):
    rows, width = local.shape
    shards = pieces.shape[0]
    tile = rows // owners // CHUNKS

    def body(my_ref, pieces_ref, local_ref, prefix_ref, branch_ref, states_ref, carry_ref, *mixed_refs):
        mine = my_ref[0]
        i = pl.program_id(0)

        @pl.when(i == 0)
        def _():
            entering = jnp.zeros((1, width), F32)
            for s in range(shards - 1):
                longer = pieces_ref[s, 0:1] * entering + pieces_ref[s, 1:2]
                entering = jnp.where(s < mine, longer, entering)
            carry_ref[...] = jnp.broadcast_to(entering, (8, width))

        states = local_ref[...] + prefix_ref[...] * carry_ref[0:1]
        states_ref[...] = states
        mixed = (states * gelu(branch_ref[...])).astype(BF16)
        for c in range(CHUNKS):

            @pl.when(i % CHUNKS == c)
            def _(c=c):
                mixed_refs[c][0] = mixed

    tiles = pl.BlockSpec((tile, width), lambda i, *_: (i, 0))
    return call(
        body,
        (rows // tile,),
        [whole(pieces.shape), tiles, tiles, tiles],
        [
            tiles,
            whole((8, width)),
        ]
        + [pl.BlockSpec((1, tile, width), lambda i, *_: (i // CHUNKS, 0, 0))] * CHUNKS,
        [struct((rows, width), F32), struct((8, width), F32)]
        + [struct((owners, tile, width), BF16)] * CHUNKS,
        prefetch=1,
        flops=60 * rows * width,
        moved=18 * rows * width,
    )(place, pieces, local, prefix, branch)


def output_rows(chunk, place, mixed_full, w_near, w_far, stream, gain, kept):
    sources, sub, width = mixed_full.shape
    own = sub * CHUNKS
    channels = w_near.shape[1]
    model = stream.shape[1]
    half = model // 2

    def body(place_ref, mixed_ref, near_ref, far_ref, stream_ref, gain_ref, *rest):
        resid_ref, rows_ref, normed_ref = rest[-3:]
        s = pl.program_id(0)
        rows_ref[...] = mixed_ref[0]
        near = pl.ds(pl.multiple_of(place_ref[2] * half, half), half)
        far = pl.ds(pl.multiple_of((1 - place_ref[2]) * half, half), half)

        @pl.when(s == 0)
        def _():
            resid_ref[...] = stream_ref[...].astype(F32)

        mixed = mixed_ref[0, :, :channels]
        resid_ref[:, near] += mm(mixed, near_ref[0])
        resid_ref[:, far] += mm(mixed, far_ref[0])

        @pl.when(s == sources - 1)
        def _():
            x = resid_ref[...]
            inv = lax.rsqrt(jnp.mean(x * x, axis=-1, keepdims=True) + EPSILON)
            normed_ref[...] = (x * inv * gain_ref[...]).astype(BF16)

    kept = tuple(kept)
    return call(
        body,
        (sources,),
        [
            pl.BlockSpec((1, sub, width), lambda s, *_: (s, 0, 0)),
            pl.BlockSpec((1, channels, half), lambda s, *_: (s, 0, 0)),
            pl.BlockSpec((1, channels, half), lambda s, *_: (s, 0, 0)),
            pl.BlockSpec((sub, model), lambda s, p: (p[1] * CHUNKS + chunk, 0)),
            whole((1, model)),
        ]
        + [pl.BlockSpec(memory_space=pl.ANY)] * len(kept),
        [
            pl.BlockSpec((sub, model), lambda s, *_: (chunk, 0)),
            pl.BlockSpec((sub, width), lambda s, *_: (chunk, s)),
            whole((sub, model)),
        ],
        [
            struct((own, model), F32),
            struct((own, sources * width), BF16),
            struct((sub, model), BF16),
        ],
        prefetch=1,
        aliases={6 + j: j for j in range(len(kept))},
        flops=2 * sources * sub * width * model,
        moved=2 * sources * width * model + 8 * sub * model,
    )(place, mixed_full, w_near, w_far, stream, gain, *kept)


def mlp_tile(hidden):
    return 256 if hidden % 256 == 0 else LANES


def mlp_chunk(chunk, place, normed, upstream, resid_own, w_gate, w_up, w_down, parts, kept):
    rows, model = normed.shape
    hidden = w_gate.shape[1]
    total = upstream.shape[0]
    sub = resid_own.shape[0] // CHUNKS
    tile = mlp_tile(hidden)
    steps = hidden // tile

    def body(place_ref, n_ref, u_ref, r_ref, wg_ref, wu_ref, wd_ref, *rest):
        act_ref, pair_ref, near_ref, far_ref, down_ref, grad_ref, down_acc, grad_acc = rest[-8:]
        s = pl.program_id(0)

        @pl.when(s == 0)
        def _():
            split_columns(near_ref, far_ref, n_ref[...], place_ref[2], parts)
            down_acc[...] = jnp.zeros_like(down_acc)
            own = pl.ds(pl.multiple_of(place_ref[1] * sub, sub), sub)
            down_acc[own, :] = r_ref[...]

        gate_pre = mm(n_ref[...], wg_ref[...])
        up_pre = mm(n_ref[...], wu_ref[...])
        inner = mm(u_ref[...], wd_ref[...], NT)
        act, slope = gelu_both(gate_pre)
        inner_act = (act * up_pre).astype(BF16)
        gate_low = (inner * up_pre * slope).astype(BF16)
        up_low = (inner * act).astype(BF16)
        act_ref[...] = inner_act
        pair_ref[:, :tile] = gate_low
        pair_ref[:, tile:] = up_low
        down_acc[...] += mm(inner_act, wd_ref[...])
        both = mm(gate_low, wg_ref[...], NT) + mm(up_low, wu_ref[...], NT)

        @pl.when(s == 0)
        def _():
            grad_acc[...] = both

        @pl.when(s > 0)
        def _():
            grad_acc[...] += both

        @pl.when(s == steps - 1)
        def _():
            down_ref[...] = down_acc[...].astype(BF16)
            grad_ref[...] = grad_acc[...].astype(BF16)

    rows_of = pl.BlockSpec((rows, model), lambda s, *_: (chunk, 0))
    kept = tuple(kept)
    return call(
        body,
        (steps,),
        [
            whole((rows, model)),
            rows_of,
            pl.BlockSpec((sub, model), lambda s, *_: (chunk, 0)),
            pl.BlockSpec((model, tile), lambda s, *_: (0, s)),
            pl.BlockSpec((model, tile), lambda s, *_: (0, s)),
            pl.BlockSpec((tile, model), lambda s, *_: (s, 0)),
        ]
        + [pl.BlockSpec(memory_space=pl.ANY)] * len(kept),
        [
            pl.BlockSpec((rows, tile), lambda s, *_: (chunk, s)),
            pl.BlockSpec((rows, 2 * tile), lambda s, *_: (chunk, s)),
            pl.BlockSpec((rows, model // 2), lambda s, *_: (chunk, 0)),
            pl.BlockSpec((rows, model // 2), lambda s, *_: (chunk, 0)),
            rows_of,
            whole((rows, model)),
        ],
        [
            struct((total, hidden), BF16),
            struct((total, 2 * hidden), BF16),
            struct((total, model // 2), BF16),
            struct((total, model // 2), BF16),
            struct((total, model), BF16),
            struct((rows, model), BF16),
        ],
        [pltpu.VMEM((rows, model), F32), pltpu.VMEM((rows, model), F32)],
        prefetch=1,
        aliases={7 + j: j for j in range(len(kept))},
        flops=12 * rows * hidden * model,
        moved=6 * hidden * model + 10 * rows * model,
    )(place, normed, upstream, resid_own, w_gate, w_up, w_down, *kept)


def resid_backward(chunk, place, normed_grad, upstream, resid_own, gain, w_near, w_far, width, parts, kept):
    sub, model = normed_grad.shape
    own = resid_own.shape[0]
    sources, channels, half = w_near.shape

    def body(place_ref, g_ref, up_ref, r_ref, gain_ref, near_ref, far_ref, *rest):
        low_near_ref, low_far_ref, rg_ref, mg_ref, sum_ref, low_ref = rest[-6:]

        @pl.when(pl.program_id(0) == 0)
        def _():
            x = r_ref[...]
            g = g_ref[...].astype(F32)
            inv = lax.rsqrt(jnp.mean(x * x, axis=-1, keepdims=True) + EPSILON)
            unit = x * inv
            scaled = g * gain_ref[...]
            dot = jnp.mean(scaled * unit, axis=-1, keepdims=True)
            grad = up_ref[...].astype(F32) + inv * (scaled - unit * dot)
            rg_ref[...] = grad
            low_ref[...] = grad.astype(BF16)
            split_columns(low_near_ref, low_far_ref, grad.astype(BF16), place_ref[2], parts)
            sum_ref[...] = jnp.sum(g * unit, axis=0, keepdims=True)

        near = pl.ds(pl.multiple_of(place_ref[2] * half, half), half)
        far = pl.ds(pl.multiple_of((1 - place_ref[2]) * half, half), half)
        if channels < width:
            mg_ref[...] = jnp.zeros_like(mg_ref)
        mg_ref[0, :, :channels] = (
            mm(low_ref[:, near], near_ref[0], NT) + mm(low_ref[:, far], far_ref[0], NT)
        ).astype(BF16)

    rows = pl.BlockSpec((sub, model), lambda s, *_: (chunk, 0))
    kept = tuple(kept)
    return call(
        body,
        (sources,),
        [
            whole((sub, model)),
            pl.BlockSpec((sub, model), lambda s, p: (chunk * sources + p[1], 0)),
            rows,
            whole((1, model)),
            pl.BlockSpec((1, channels, half), lambda s, *_: (s, 0, 0)),
            pl.BlockSpec((1, channels, half), lambda s, *_: (s, 0, 0)),
        ]
        + [pl.BlockSpec(memory_space=pl.ANY)] * len(kept),
        [
            pl.BlockSpec((sub, half), lambda s, *_: (chunk, 0)),
            pl.BlockSpec((sub, half), lambda s, *_: (chunk, 0)),
            rows,
            pl.BlockSpec((1, sub, width), lambda s, *_: (s, chunk, 0)),
            whole((1, model)),
        ],
        [
            struct((own, half), BF16),
            struct((own, half), BF16),
            struct((own, model), F32),
            struct((sources, own, width), BF16),
            struct((1, model), F32),
        ],
        [pltpu.VMEM((sub, model), BF16)],
        prefetch=1,
        aliases={7 + j: j for j in range(len(kept))},
        flops=2 * sources * sub * width * model,
        moved=2 * sources * width * model + 14 * sub * model,
    )(place, normed_grad, upstream, resid_own, gain, w_near, w_far, *kept)


def recurrent_back_scan(mixed_grad, branch, keep, tail):
    rows, width = branch.shape
    tile = 256
    tiles_n = rows // tile

    def body(mg_ref, branch_ref, keep_ref, tail_ref, grad_ref, after_ref, edge_ref, ext, carry):
        i = pl.program_id(0)

        @pl.when(i == 0)
        def _():
            ext[tile : tile + 8] = jnp.ones((8, width), F32)
            carry[0:1] = jnp.ones((1, width), F32)
            carry[1:2] = jnp.zeros((1, width), F32)

        @pl.when(i > 0)
        def _():
            ext[tile : tile + 8] = ext[0:8]

        ext[0:tile] = keep_ref[...]
        for lane in range(0, width, LANES):
            cut = slice(lane, lane + LANES)
            direct = mg_ref[:, cut].astype(F32) * gelu(branch_ref[:, cut])
            keeps, grads, keep_out, grad_out = tile_scan(
                ext[1 : tile + 1, cut], direct, carry[0:1, cut], carry[1:2, cut], True
            )
            grad_ref[:, cut] = grads
            after_ref[:, cut] = keeps
            carry[0:1, cut] = keep_out
            carry[1:2, cut] = grad_out

        @pl.when(i == tiles_n - 1)
        def _():
            edge_ref[0:1] = tail_ref[0:1]
            edge_ref[1:2] = keep_ref[0:1] * carry[1:2]
            edge_ref[2:8] = jnp.zeros((6, width), F32)

    tiles = pl.BlockSpec((tile, width), lambda i: (tiles_n - 1 - i, 0))
    return call(
        body,
        (tiles_n,),
        [tiles, tiles, tiles, whole((8, width))],
        [tiles, tiles, whole((8, width))],
        [struct((rows, width), F32), struct((rows, width), F32), struct((8, width), F32)],
        [pltpu.VMEM((tile + 8, width), F32), pltpu.VMEM((8, width), F32)],
        flops=100 * rows * width,
        moved=18 * rows * width,
    )(mixed_grad, branch, keep, tail)


def recurrent_backward(
    place, pieces, local_grad, after_keep, mixed_grad, branch, states, carry_in, pre, conv_low,
    dist, inputs, halo, conv_weight, decay, gate_weights,
):
    rows, width = branch.shape
    shards = pieces.shape[0]
    tile = 256
    tiles_n = rows // tile
    blocks = tile // 8

    def body(
        place_ref, pieces_ref, lg_ref, ak_ref, mg_ref, branch_ref, states_ref, before_ref, carry_ref,
        pre_ref, conv_ref, dist_ref, in_ref, in_before_ref, halo_ref, cw_ref, dp_ref, gw_ref,
        bl_ref, il_ref, pl_ref, sums_ref, end_ref, edge_ref,
        back, prev, ext, acc, cg,
    ):
        i = pl.program_id(0)
        mine = place_ref[0]

        @pl.when(i == 0)
        def _():
            entering = jnp.zeros((1, width), F32)
            for s in range(shards - 1, 0, -1):
                longer = pieces_ref[s, 0:1] * entering + pieces_ref[s, 1:2]
                entering = jnp.where(s > mine, longer, entering)
            back[...] = jnp.broadcast_to(entering, (8, width))
            sums_ref[...] = jnp.zeros_like(sums_ref)
            acc[tile : tile + 16] = jnp.zeros((16, width), F32)

        @pl.when(i > 0)
        def _():
            acc[tile : tile + 8] = acc[0:8]
            acc[tile + 8 : tile + 16] = jnp.zeros((8, width), F32)

        @pl.when(i == tiles_n - 1)
        def _():
            prev[0:8] = carry_ref[...]
            ext[0:8] = halo_ref[...]

        @pl.when(i < tiles_n - 1)
        def _():
            prev[0:8] = before_ref[...]
            ext[0:8] = in_before_ref[...]

        prev[8 : 8 + tile] = states_ref[...]
        ext[8 : 8 + tile] = in_ref[...]
        acc[0:tile] = jnp.zeros((tile, width), F32)
        dist = dist_ref[...]
        notstart = dist > 0
        for lane in range(0, width, LANES):
            cut = slice(lane, lane + LANES)
            far = slice(width + lane, width + lane + LANES)
            grad = lg_ref[:, cut] + ak_ref[:, cut] * back[0:1, cut]
            _, slope = gelu_both(branch_ref[:, cut])
            bl_ref[:, cut] = (mg_ref[:, cut].astype(F32) * states_ref[:, cut] * slope).astype(BF16)
            reset = sigmoid(pre_ref[:, cut])
            gate = sigmoid(pre_ref[:, far])
            power = -GATE_POWER * softplus_neg(dp_ref[:, cut])
            keep = jnp.exp(power * reset)
            inside = 1.0 - keep * keep + ROOT_FLOOR
            unroot = lax.rsqrt(inside)
            root = inside * unroot
            conv = conv_ref[:, cut].astype(F32)
            through = gate * conv
            keep_grad = jnp.where(notstart, grad * prev[7 : 7 + tile, cut], 0.0) - grad * through * (
                keep * unroot
            )
            kg = keep_grad * keep * reset
            pl_ref[:, cut] = (kg * power * (1.0 - reset)).astype(BF16)
            rooted = grad * root
            cg[:, cut] = rooted * gate
            pl_ref[:, far] = (rooted * through * (1.0 - gate)).astype(BF16)
            sums_ref[40:48, cut] += jnp.sum(kg.reshape(blocks, 8, LANES), axis=0)
        cg[...] += mm(pl_ref[...], gw_ref[...], NT)
        for lane in range(0, width, LANES):
            cut = slice(lane, lane + LANES)
            conv_grad = cg[:, cut]
            sums_ref[32:40, cut] += jnp.sum(conv_grad.reshape(blocks, 8, LANES), axis=0)
            for k in range(CONV):
                masked = conv_grad if k == 0 else jnp.where(dist >= k, conv_grad, 0.0)
                tap = masked * ext[8 - k : 8 - k + tile, cut]
                sums_ref[8 * k : 8 * k + 8, cut] += jnp.sum(tap.reshape(blocks, 8, LANES), axis=0)
                acc[8 - k : 8 - k + tile, cut] += cw_ref[k : k + 1, cut] * masked
        il_ref[...] = acc[8 : 8 + tile].astype(BF16)

        @pl.when(i == 0)
        def _():
            end_ref[...] = acc[tile : tile + 8]

        @pl.when(i == tiles_n - 1)
        def _():
            edge_ref[...] = acc[0:8]

    tiles = pl.BlockSpec((tile, width), lambda i, *_: (tiles_n - 1 - i, 0))
    wide = pl.BlockSpec((tile, 2 * width), lambda i, *_: (tiles_n - 1 - i, 0))
    before = pl.BlockSpec(
        (8, width), lambda i, *_: (jnp.maximum((tiles_n - 1 - i) * blocks - 1, 0), 0)
    )
    small = whole((8, width))
    return call(
        body,
        (tiles_n,),
        [
            whole(pieces.shape), tiles, tiles, tiles, tiles, tiles, before, small, wide, tiles,
            pl.BlockSpec((tile, 1), lambda i, *_: (tiles_n - 1 - i, 0)),
            tiles, before, small, whole((CONV, width)), whole((1, width)), whole((width, 2 * width)),
        ],
        [tiles, tiles, wide, whole((48, width)), small, small],
        [
            struct((rows, 2 * width), BF16),
            struct((rows, width), BF16),
            struct((rows, 2 * width), BF16),
            struct((48, width), F32),
            struct((8, width), F32),
            struct((8, width), F32),
        ],
        [
            pltpu.VMEM((8, width), F32),
            pltpu.VMEM((tile + 8, width), F32),
            pltpu.VMEM((tile + 8, width), F32),
            pltpu.VMEM((tile + 16, width), F32),
            pltpu.VMEM((tile, width), F32),
        ],
        prefetch=1,
        flops=4 * rows * width * width + 300 * rows * width,
        moved=40 * rows * width,
    )(
        place, pieces, local_grad, after_keep, mixed_grad, branch, states, states, carry_in, pre,
        conv_low, dist, inputs, inputs, halo, conv_weight, decay, gate_weights,
    )


def input_backward(place, rec_low, inputs_low, end, returned, w_branch, w_input, stream, gain, resid_grad):
    rows, width = inputs_low.shape
    channels = w_branch.shape[0]
    model = stream.shape[1]
    tile = resid_grad.shape[0]
    steps = rows // tile

    def body(
        place_ref, bl_ref, il_ref, end_ref, ret_ref, wb_ref, wi_ref, x_ref, gain_ref, rg_ref,
        part_ref, fixed_ref, sum_ref,
    ):
        i = pl.program_id(0)
        fixed_ref[...] = il_ref[...]

        @pl.when(i == steps - 1)
        def _():
            tail = jnp.concatenate(
                [il_ref[tile - 16 : tile - 8].astype(F32), end_ref[...] + ret_ref[...]], axis=0
            )
            fixed_ref[tile - 16 : tile] = tail.astype(BF16)

        g = mm(bl_ref[:, :channels], wb_ref[...]) + mm(fixed_ref[:, :channels], wi_ref[...])
        x = x_ref[...].astype(F32)
        inv = lax.rsqrt(jnp.mean(x * x, axis=-1, keepdims=True) + EPSILON)
        unit = x * inv
        scaled = g * gain_ref[...]
        dot = jnp.mean(scaled * unit, axis=-1, keepdims=True)
        part = inv * (scaled - unit * dot)
        sums = jnp.sum(g * unit, axis=0, keepdims=True)

        @pl.when(i == 0)
        def _():
            sum_ref[...] = sums

        @pl.when(i > 0)
        def _():
            sum_ref[...] += sums

        @pl.when(i == place_ref[1])
        def _():
            part_ref[...] = (part + rg_ref[...]).astype(BF16)

        @pl.when(i != place_ref[1])
        def _():
            part_ref[...] = part.astype(BF16)

    tiles = pl.BlockSpec((tile, width), lambda i, *_: (i, 0))
    wide = pl.BlockSpec((tile, model), lambda i, *_: (i, 0))
    return call(
        body,
        (steps,),
        [
            tiles, tiles, whole((8, width)), whole((8, width)), whole((channels, model)), whole((channels, model)), wide,
            whole((1, model)), whole((tile, model)),
        ],
        [wide, pl.BlockSpec((tile, width), lambda i, *_: (i, 1)), whole((1, model))],
        [struct((rows, model), BF16), struct((rows, 2 * width), BF16), struct((1, model), F32)],
        prefetch=1,
        aliases={1: 1},
        flops=4 * rows * width * model + 30 * rows * model,
        moved=4 * rows * model + 4 * width * model + 6 * rows * width,
    )(place, rec_low, inputs_low, end, returned, w_branch, w_input, stream, gain, resid_grad)


def gate_gradients(conv_low, pre_low, extra, heads):
    rows, width = conv_low.shape
    size = extra.shape[0]

    def body(conv_ref, pre_ref, extra_ref, out_ref, full):
        full[...] = mm(conv_ref[...], pre_ref[...], TN)
        for g in range(2):
            for h in range(heads):
                at = h * size
                out_ref[g * heads + h] = full[at : at + size, g * width + at : g * width + at + size]
        out_ref[2 * heads] = extra_ref[...]

    return call(
        body,
        (1,),
        [whole((rows, width)), whole((rows, 2 * width)), whole((size, size))],
        whole((2 * heads + 1, size, size)),
        struct((2 * heads + 1, size, size), F32),
        [pltpu.VMEM((width, 2 * width), F32)],
        flops=4 * rows * width * width,
        moved=6 * rows * width,
    )(conv_low, pre_low, extra)


def block_diagonal(blocks, width):
    heads, size = blocks.shape[0], blocks.shape[1]
    rows = [
        jnp.pad(blocks[h], ((0, 0), (h * size, width - (h + 1) * size))) for h in range(heads)
    ]
    return jnp.pad(jnp.concatenate(rows, axis=0), ((0, width - heads * size), (0, 0)))


def shards(
    tokens,
    cotangent,
    destination,
    lengths,
    norm_gain,
    w_branch,
    w_input,
    conv_weight,
    conv_bias,
    w_recur,
    w_ingate,
    decay_param,
    w_out,
    mlp_gain,
    w_gate,
    w_up,
    w_down,
):
    shard_count = lax.axis_size("seq")
    my_shard = lax.axis_index("seq")
    model_count = lax.axis_size("mp")
    my_model = lax.axis_index("mp")
    row_count, model_width = tokens.shape
    slab_width = model_width // model_count
    per_peer = row_count // shard_count
    own_rows = row_count // model_count
    sub = own_rows // CHUNKS
    channels = w_branch.shape[1]
    heads, block_width = w_recur.shape[0], w_recur.shape[1]
    width = -(-channels // LANES) * LANES
    parity = my_shard % 2
    place = jnp.stack([my_shard, my_model, parity]).astype(jnp.int32)
    pad_lanes = functools.partial(jnp.pad, pad_width=((0, 0), (0, width - channels)))

    bits = shard_count.bit_length() - 1

    def scatter_sum(x, axis, dim):
        return lax.psum_scatter(x, axis, scatter_dimension=dim, tiled=True)

    def exchange(x, axis):
        return lax.all_to_all(x, axis, split_axis=0, concat_axis=0, tiled=True)

    def swap(x, bit):
        return lax.ppermute(x, "seq", [(i, i ^ (1 << bit)) for i in range(shard_count)])

    def add_low(left, right):
        return (left.astype(F32) + right.astype(F32)).astype(BF16)

    def tie(*values):
        return lax.optimization_barrier(values)

    def halves(x, up):
        done = bits - x.shape[0].bit_length() + 1
        bit = done if up else bits - done
        mine = (my_shard >> bit) & 1
        axis = 1 if up else 0
        x = x.reshape(-1, 2, *x.shape[1:]) if up else x.reshape(2, -1, *x.shape[1:])
        return bit, [lax.dynamic_index_in_dim(x, m, axis, False) for m in (mine, 1 - mine)]

    def others(pair):
        return [halves(x, up)[1][1] for x, up in zip(pair, (True, False))]

    def send_others(pair, made):
        return [swap(o, halves(x, up)[0]) for x, up, o in zip(pair, (True, False), made)]

    def send_all(pair):
        return send_others(pair, others(pair))

    def add_all(pair, received):
        return [add_low(halves(x, up)[1][0], r) for x, up, r in zip(pair, (True, False), received)]

    local_dest = lax.dynamic_slice_in_dim(destination, my_shard * row_count, row_count)
    dest_row, dest_col = local_dest.reshape(1, -1), local_dest.reshape(-1, 1)
    straight = jnp.zeros((1,), jnp.int32)
    turn = (my_shard * per_peer).astype(jnp.int32)[None]
    w_gates = jnp.concatenate(
        [block_diagonal(w_recur, width), block_diagonal(w_ingate, width)], axis=1
    )
    sent_tokens, w_gates, cotangent = tie(
        send_order(straight, dest_row, dest_col, tokens), w_gates, cotangent
    )
    arrived_tokens = exchange(sent_tokens, "seq")
    cot_blocks = send_blocks(turn, dest_row, dest_col, cotangent, shard_count)
    sorted_dest = jnp.sort(destination.reshape(shard_count, row_count), axis=1)
    landing = (
        lax.dynamic_slice_in_dim(sorted_dest, my_shard * per_peer, per_peer, 1).reshape(-1)
        - my_shard * row_count
    )
    landing_row = landing.reshape(1, -1)
    turned = jnp.stack(
        [
            lax.dynamic_index_in_dim(landing.reshape(shard_count, per_peer), my_shard ^ k, 0, False)
            for k in range(shard_count)
        ]
    ).reshape(1, -1)
    cot_other = swap(jnp.concatenate(cot_blocks[1::2], axis=0), 0).reshape(-1, per_peer, model_width)
    sent_cot = [
        jnp.concatenate([cot_blocks[2 * q], cot_other[q]], axis=0) for q in range(shard_count // 2)
    ]
    mlp_place = np.arange(row_count, dtype=np.int32).reshape(model_count, CHUNKS, sub)
    mlp_place = jnp.asarray(mlp_place.transpose(1, 0, 2).reshape(-1, 1))
    mlp_landing = (
        (landing % own_rows) // sub * (model_count * sub) + landing // own_rows * sub + landing % sub
    )

    positions = my_shard * row_count + jnp.arange(row_count, dtype=jnp.int32)
    count = lengths.shape[0]
    earlier = np.tril(np.ones((count, count), np.int32), -1)
    seq_starts = jnp.sum(jnp.asarray(earlier) * lengths[None, :], axis=1)
    seq_start = jnp.max(
        jnp.where(seq_starts[None, :] <= positions[:, None], seq_starts[None, :], 0), axis=1
    )
    dist = (positions - seq_start).reshape(-1, 1)

    w_branch, w_input = w_branch.T, w_input.T
    taps = pad_lanes(conv_weight)
    bias = pad_lanes(conv_bias[None])
    decay = pad_lanes(decay_param[None])
    gain = norm_gain[None]
    gain2 = mlp_gain[None]
    half = model_width // 2
    w_out_half = jnp.pad(
        lax.dynamic_slice_in_dim(w_out, parity * half, half, 1), ((0, -channels % 16), (0, 0))
    )
    w_near = lax.all_gather(w_out_half, "mp", axis=0)

    arrived_tokens, w_gates, *sent_cot = tie(arrived_tokens, w_gates, *sent_cot)
    stream, hidden_near, hidden_far, branch, inputs = project(
        place, landing_row, arrived_tokens, gain, w_branch, w_input, width, shard_count
    )
    halo = lax.ppermute(
        inputs[row_count - 8 :], "seq", [(i, i + 1) for i in range(shard_count - 1)]
    )
    conv_low, pre, keep, prefix, local, tail = recurrent_forward(
        inputs, halo, dist, taps, bias, decay, w_gates
    )
    pieces = lax.all_gather(tail, "seq")
    pieces, *sent_cot = tie(pieces, *sent_cot)
    cot_blocks = [sent_cot[0]] + [
        lax.ppermute(sent_cot[q], "seq", [(i, i ^ (2 * q)) for i in range(shard_count)])
        for q in range(1, shard_count // 2)
    ]
    states, carry_in, *mixed = finish_states(
        place, pieces, local, prefix, branch, model_count
    )
    mixed[0], w_near = tie(mixed[0], w_near)
    w_far = swap(w_near, 0)

    rows_kept, normeds = (), []
    for c in range(CHUNKS):
        mixed_full = exchange(mixed[c], "mp")
        if c == 0:
            mixed_full, *cot_blocks[1:3] = tie(mixed_full, *cot_blocks[1:3])
        *rows_kept, normed_own = output_rows(
            c, place, mixed_full, w_near, w_far, stream, gain2, rows_kept
        )
        normeds.append(normed_own)
    resid_own, mixed_rows = rows_kept
    normeds[-1], *cot_blocks = tie(normeds[-1], *cot_blocks)
    upstream, upstream_near, upstream_far = place_upstream(
        place, mlp_place, turned, cot_blocks, shard_count
    )
    kept, grads = (), []
    for c in range(CHUNKS):
        if c == 0:
            normed = lax.all_gather(normeds[c], "mp", axis=0, tiled=True)
        else:
            normed = exchange(
                jnp.broadcast_to(normeds[c], (model_count, *normeds[c].shape)), "mp"
            ).reshape(-1, model_width)
        *kept, grad = mlp_chunk(
            c, place, normed, upstream, resid_own, w_gate, w_up, w_down, shard_count, kept
        )
        grads.append(scatter_sum(grad, "mp", 0))
    inner_act, pair_low, normed_near, normed_far, block_part = kept

    parts = shard_count // 2
    part_width = model_width // shard_count
    hidden_units = w_gate.shape[1]

    def outer(left, right):
        return mm(left, right, TN).astype(BF16)

    def with_partner(near, sent, right):
        return (mm(near, right, TN) + sent.astype(F32)).astype(BF16).reshape(
            parts, part_width, right.shape[1]
        )

    def two_ways(x):
        cut = x.shape[2] // 2
        return [x[..., :cut], x[..., cut:]]

    def finish(pair):
        while pair[0].shape[0] > 1:
            pair = add_all(pair, send_all(pair))
        return jnp.concatenate([x[0] for x in pair], axis=1)

    far_pair = outer(normed_far, pair_low)
    far_down = outer(upstream_far, inner_act)
    grads[0], far_pair, far_down = tie(grads[0], far_pair, far_down)
    far_pair, far_down = swap(far_pair, 0), swap(far_down, 0)

    def second_norm(c, kept):
        return resid_backward(
            c, place, grads[c], upstream, resid_own, gain2, w_near, w_far, width, shard_count, kept
        )

    *lows, gain_first = second_norm(0, ())
    lows[0], pair_low = tie(lows[0], pair_low)
    grad_pair = with_partner(normed_near, far_pair, pair_low)
    grad_pair, inner_act = tie(grad_pair, inner_act)
    pair = two_ways(grad_pair)
    pair_received = send_all(pair)
    down = two_ways(with_partner(upstream_near, far_down, inner_act))
    grads[1], *down = tie(grads[1], *down)
    near_low, far_low, resid_grad, mixed_grad_full, gain_second = second_norm(1, lows)
    mlp_gain_part = gain_first + gain_second
    mixed_grad = exchange(mixed_grad_full.reshape(row_count, width), "mp")
    far_out = outer(far_low, mixed_rows)
    far_out, *pair_received = tie(far_out, *pair_received)
    pair = add_all(pair, pair_received)
    pair_received = send_all(pair)
    mixed_grad, far_out, block_part, *pair_received = tie(
        mixed_grad, far_out, block_part, *pair_received
    )
    far_out = swap(far_out, 0)
    block_share = scatter_sum(block_part, "mp", 1)

    local_grad, after_keep, edge_pair = recurrent_back_scan(mixed_grad, branch, keep, tail)
    back_pieces = lax.all_gather(edge_pair, "seq")
    back_pieces, *down = tie(back_pieces, *down)
    down_received = send_all(down)
    rec_low, inputs_part, pre_low, sums, end, edge = recurrent_backward(
        place, back_pieces, local_grad, after_keep, mixed_grad, branch, states, carry_in, pre,
        conv_low, dist, inputs, halo, taps, decay, w_gates,
    )
    edge, far_out, near_low, *down_received = tie(edge, far_out, near_low, *down_received)
    returned = lax.ppermute(edge, "seq", [(i + 1, i) for i in range(shard_count - 1)])
    out = two_ways(with_partner(near_low, far_out, mixed_rows))
    out_others = others(out)
    returned, out, out_others = tie(returned, out, out_others)
    out_received = send_others(out, out_others)
    input_part, rec_low, norm_gain_part = input_backward(
        place, rec_low, inputs_part, end, returned, w_branch, w_input, stream, gain, resid_grad
    )
    input_part, block_share, pre_low, pair, down, pair_received, down_received, *out_received = tie(
        input_part, block_share, pre_low, pair, down, pair_received, down_received, *out_received
    )
    input_share = scatter_sum(input_part, "mp", 1)

    far_rec = swap(outer(hidden_far, rec_low), 0)

    sums = jnp.sum(sums.reshape(CONV + 2, 8, width), axis=1)[:, :channels]
    sums = jnp.concatenate(
        [sums[: CONV + 1], sums[CONV + 1 :] * (GATE_POWER * jax.nn.sigmoid(-decay_param))], axis=0
    )
    gains = jnp.concatenate([norm_gain_part, mlp_gain_part], axis=0)
    gains = gains.reshape(2, model_count, slab_width).transpose(1, 0, 2)
    gains = jnp.sum(exchange(gains, "mp"), axis=0)
    sum_rows = sums.size // block_width
    gain_rows = -(-gains.size // block_width)
    gains = jnp.pad(gains.reshape(-1), (0, gain_rows * block_width - gains.size))
    extra = jnp.concatenate(
        [sums.reshape(sum_rows, block_width), gains.reshape(gain_rows, block_width)], axis=0
    )
    extra = jnp.pad(extra, ((0, block_width - sum_rows - gain_rows), (0, 0)))
    small = gate_gradients(conv_low, pre_low, extra, heads)
    small, hidden_near = tie(small, hidden_near)
    small = lax.psum(small, "seq")
    sums = small[2 * heads, :sum_rows].reshape(CONV + 2, channels)
    gains = small[2 * heads, sum_rows : sum_rows + gain_rows].reshape(-1)
    gains = gains[: 2 * slab_width].reshape(2, slab_width)

    out = add_all(out, out_received)
    grad_rec = with_partner(hidden_near, far_rec, rec_low)
    block_share, grad_rec = tie(block_share, grad_rec)
    sent_rec = finish(two_ways(grad_rec))
    sent_out = finish(out)
    sent_branch = sent_rec[:, :channels].astype(F32)
    sent_input = sent_rec[:, width : width + channels].astype(F32)
    all_rows = jnp.arange(row_count, dtype=jnp.int32)[None]
    home_block = exchange(place_rows(mlp_landing.reshape(-1, 1), all_rows, block_share), "seq")
    sent_pair = finish(add_all(pair, pair_received))
    sent_down = finish(add_all(down, down_received)).astype(F32).T
    unit = mlp_tile(hidden_units)
    sent_pair = sent_pair.reshape(part_width, hidden_units // unit, 2, unit)
    sent_gate = sent_pair[:, :, 0].reshape(part_width, hidden_units).astype(F32)
    sent_up = sent_pair[:, :, 1].reshape(part_width, hidden_units).astype(F32)
    input_share, home_block, sent_gate, sent_up, sent_down = tie(
        input_share, home_block, sent_gate, sent_up, sent_down
    )
    sent_out = scatter_sum(sent_out, "mp", 1)
    sent_out = sent_out[:, :channels].astype(F32).T

    home_input = exchange(place_rows(landing.reshape(-1, 1), all_rows, input_share), "seq")
    block_out = restore_rows(dest_row, dest_col, home_block)
    input_grad = restore_rows(dest_row, dest_col, home_input)
    return (
        block_out,
        input_grad,
        gains[0],
        sent_branch,
        sent_input,
        sums[:CONV],
        sums[CONV],
        small[:heads],
        small[heads : 2 * heads],
        sums[CONV + 1],
        sent_out,
        gains[1],
        sent_gate,
        sent_up,
        sent_down,
    )


def solution(mesh):
    in_specs = (
        P("seq", None),
        P("seq", None),
        P(),
        P(),
        P(),
        P(None, "mp"),
        P(None, "mp"),
        P(None, "mp"),
        P("mp"),
        P("mp", None, None),
        P("mp", None, None),
        P("mp"),
        P("mp", None),
        P(),
        P(None, "mp"),
        P(None, "mp"),
        P("mp", None),
    )
    out_specs = (
        P("seq", "mp"),
        P("seq", "mp"),
        P("mp"),
        P("seq", "mp"),
        P("seq", "mp"),
        P(None, "mp"),
        P("mp"),
        P("mp", None, None),
        P("mp", None, None),
        P("mp"),
        P("mp", "seq"),
        P("mp"),
        P("seq", "mp"),
        P("seq", "mp"),
        P("mp", "seq"),
    )
    return jax.shard_map(shards, mesh=mesh, in_specs=in_specs, out_specs=out_specs, check_vma=False)
```

```python
import functools

import jax
import jax.numpy as jnp
import numpy as np
from jax import lax
from jax.experimental import pallas as pl
from jax.experimental.pallas import tpu as pltpu
from jax.sharding import PartitionSpec as P

CONV = 4
EPSILON = 1e-06
GATE_POWER = 8.0
ROOT_FLOOR = 0.01
LANES = 128
GROUP = 8
CHUNKS = 2
F32 = jnp.float32
BF16 = jnp.bfloat16
MIB = 1 << 20
GELU_A = 0.7978845608028654
GELU_B = 0.044715

NN = (((1,), (0,)), ((), ()))
NT = (((1,), (1,)), ((), ()))
TN = (((0,), (0,)), ((), ()))


def mm(left, right, dims=NN):
    return lax.dot_general(left, right, dims, preferred_element_type=F32)


def call(body, grid, in_specs, out_specs, out_shape, scratch=(), prefetch=0, aliases=None, flops=0, moved=0):
    return pl.pallas_call(
        body,
        grid_spec=pltpu.PrefetchScalarGridSpec(
            num_scalar_prefetch=prefetch,
            grid=grid,
            in_specs=in_specs,
            out_specs=out_specs,
            scratch_shapes=list(scratch),
        ),
        out_shape=out_shape,
        input_output_aliases=aliases or {},
        compiler_params=pltpu.CompilerParams(
            dimension_semantics=("arbitrary",) * len(grid), vmem_limit_bytes=60 * MIB
        ),
        cost_estimate=pl.CostEstimate(
            flops=flops, bytes_accessed=moved, transcendentals=0
        ),
    )


def whole(shape):
    zeros = (0,) * len(shape)
    return pl.BlockSpec(shape, lambda *_: zeros)


def struct(shape, dtype):
    return jax.ShapeDtypeStruct(shape, dtype)


def sigmoid(x):
    return 0.5 * jnp.tanh(0.5 * x) + 0.5


def gelu(x):
    return 0.5 * x * (1.0 + jnp.tanh(GELU_A * (x + GELU_B * x * x * x)))


def gelu_both(x):
    square = x * x
    t = jnp.tanh(GELU_A * x * (1.0 + GELU_B * square))
    half = 0.5 * (1.0 + t)
    slope = half + 0.5 * x * (1.0 - t * t) * (GELU_A * (1.0 + 3.0 * GELU_B * square))
    return x * half, slope


def softplus_neg(x):
    return jnp.log1p(jnp.exp(-jnp.abs(x))) + jnp.maximum(-x, 0.0)


def one_hot(rows, lanes):
    return jnp.where(rows == lanes, 1.0, 0.0).astype(BF16)


def send_order(turn, dest_row, dest_col, values):
    rows, width = values.shape
    tile = 256

    def body(turn_ref, row_ref, col_ref, val_ref, out_ref, rank_ref):
        i = pl.program_id(0)

        @pl.when(i == 0)
        def _():
            before = jnp.where(col_ref[...] < row_ref[...], 1.0, 0.0)
            rank = jnp.sum(before, axis=0, keepdims=True).astype(jnp.int32)
            rank_ref[...] = rank ^ turn_ref[0]

        place = lax.broadcasted_iota(jnp.int32, (tile, rows), 0) + i * tile
        out_ref[...] = mm(one_hot(place, rank_ref[...]), val_ref[...]).astype(BF16)

    return call(
        body,
        (rows // tile,),
        [whole((1, rows)), whole((rows, 1)), whole((rows, width))],
        pl.BlockSpec((tile, width), lambda i, *_: (i, 0)),
        struct((rows, width), BF16),
        [pltpu.VMEM((1, rows), jnp.int32)],
        prefetch=1,
        flops=2 * rows * rows * width,
        moved=4 * rows * width,
    )(turn, dest_row, dest_col, values)


def send_blocks(turn, dest_row, dest_col, values, count):
    rows, width = values.shape
    size = rows // count

    def body(turn_ref, row_ref, col_ref, val_ref, *refs):
        rank_ref = refs[count]
        i = pl.program_id(0)

        @pl.when(i == 0)
        def _():
            before = jnp.where(col_ref[...] < row_ref[...], 1.0, 0.0)
            rank = jnp.sum(before, axis=0, keepdims=True).astype(jnp.int32)
            rank_ref[...] = rank ^ turn_ref[0]

        spot = lax.broadcasted_iota(jnp.int32, (size, rows), 0) + i * size
        moved = mm(one_hot(spot, rank_ref[...]), val_ref[...]).astype(BF16)
        for k in range(count):

            @pl.when(i == k)
            def _(k=k):
                refs[k][...] = moved

    return call(
        body,
        (count,),
        [whole((1, rows)), whole((rows, 1)), whole((rows, width))],
        [whole((size, width))] * count,
        [struct((size, width), BF16)] * count,
        [pltpu.VMEM((1, rows), jnp.int32)],
        prefetch=1,
        flops=2 * rows * rows * width,
        moved=4 * rows * width,
    )(turn, dest_row, dest_col, values)


def place_rows(place_col, landing_row, values):
    rows, width = values.shape
    tile = 256

    def body(place_ref, land_ref, val_ref, out_ref):
        out_ref[...] = mm(one_hot(place_ref[...], land_ref[...]), val_ref[...]).astype(out_ref.dtype)

    return call(
        body,
        (rows // tile,),
        [pl.BlockSpec((tile, 1), lambda i: (i, 0)), whole((1, rows)), whole((rows, width))],
        pl.BlockSpec((tile, width), lambda i: (i, 0)),
        struct((rows, width), BF16),
        flops=2 * rows * rows * width,
        moved=4 * rows * width,
    )(place_col, landing_row, values)


def split_columns(near_ref, far_ref, values, parity, parts):
    size = values.shape[1] // parts
    for q in range(parts // 2):
        to = slice(q * size, (q + 1) * size)
        even = values[:, 2 * q * size : (2 * q + 1) * size]
        odd = values[:, (2 * q + 1) * size : (2 * q + 2) * size]
        near_ref[:, to] = jnp.where(parity == 0, even, odd)
        far_ref[:, to] = jnp.where(parity == 0, odd, even)


def place_upstream(place, place_col, landing_row, blocks, parts):
    count = len(blocks)
    size, width = blocks[0].shape
    rows = count * size
    tile = 256

    def body(my_ref, place_ref, land_ref, *refs):
        out_ref, near_ref, far_ref, val_ref, sem = refs[count:]

        @pl.when(pl.program_id(0) == 0)
        def _():
            copies = [
                pltpu.make_async_copy(refs[k], val_ref.at[k * size : (k + 1) * size], sem.at[k])
                for k in range(count)
            ]
            for copy in copies:
                copy.start()
            for copy in copies:
                copy.wait()

        moved = mm(one_hot(place_ref[...], land_ref[...]), val_ref[...]).astype(BF16)
        out_ref[...] = moved
        split_columns(near_ref, far_ref, moved, my_ref[2], parts)

    return call(
        body,
        (rows // tile,),
        [pl.BlockSpec((tile, 1), lambda i, *_: (i, 0)), whole((1, rows))]
        + [pl.BlockSpec(memory_space=pl.ANY)] * count,
        [
            pl.BlockSpec((tile, width), lambda i, *_: (i, 0)),
            pl.BlockSpec((tile, width // 2), lambda i, *_: (i, 0)),
            pl.BlockSpec((tile, width // 2), lambda i, *_: (i, 0)),
        ],
        [
            struct((rows, width), BF16),
            struct((rows, width // 2), BF16),
            struct((rows, width // 2), BF16),
        ],
        [pltpu.VMEM((rows, width), BF16), pltpu.SemaphoreType.DMA((count,))],
        prefetch=1,
        flops=2 * rows * rows * width,
        moved=6 * rows * width,
    )(place, place_col, landing_row, *blocks)


def restore_rows(dest_row, dest_col, values):
    rows, width = values.shape
    tile = 256

    def body(row_ref, col_ref, val_ref, out_ref):
        before = jnp.where(row_ref[...] < col_ref[...], 1.0, 0.0)
        rank = jnp.sum(before, axis=1, keepdims=True).astype(jnp.int32)
        spot = lax.broadcasted_iota(jnp.int32, (tile, rows), 1)
        out_ref[...] = mm(one_hot(spot, rank), val_ref[...])

    return call(
        body,
        (rows // tile,),
        [whole((1, rows)), pl.BlockSpec((tile, 1), lambda i: (i, 0)), whole((rows, width))],
        pl.BlockSpec((tile, width), lambda i: (i, 0)),
        struct((rows, width), F32),
        flops=2 * rows * rows * width,
        moved=6 * rows * width,
    )(dest_row, dest_col, values)


def project(place, landing_row, arrived, gain, w_branch, w_input, half, parts):
    rows, width = arrived.shape
    channels = w_branch.shape[0]
    wide = 2 * half
    tile = 256

    def body(
        my_ref, land_ref, arr_ref, gain_ref, wb_ref, wi_ref, stream_ref, near_ref, far_ref, branch_ref, inputs_ref
    ):
        i = pl.program_id(0)
        place = lax.broadcasted_iota(jnp.int32, (tile, rows), 0) + i * tile
        x = mm(one_hot(place, land_ref[...]), arr_ref[...])
        stream_ref[...] = x.astype(BF16)
        inv = lax.rsqrt(jnp.mean(x * x, axis=-1, keepdims=True) + EPSILON)
        hidden = (x * inv * gain_ref[...]).astype(BF16)
        split_columns(near_ref, far_ref, hidden, my_ref[2], parts)
        for out_ref, w_ref in ((branch_ref, wb_ref), (inputs_ref, wi_ref)):
            if channels < half:
                out_ref[...] = jnp.zeros_like(out_ref)
            out_ref[:, :channels] = mm(hidden, w_ref[...], NT)

    return call(
        body,
        (rows // tile,),
        [whole((1, rows)), whole((rows, width)), whole((1, width))] + [whole((channels, width))] * 2,
        [
            pl.BlockSpec((tile, width), lambda i, *_: (i, 0)),
            pl.BlockSpec((tile, width // 2), lambda i, *_: (i, 0)),
            pl.BlockSpec((tile, width // 2), lambda i, *_: (i, 0)),
            pl.BlockSpec((tile, half), lambda i, *_: (i, 0)),
            pl.BlockSpec((tile, half), lambda i, *_: (i, 0)),
        ],
        [
            struct((rows, width), BF16),
            struct((rows, width // 2), BF16),
            struct((rows, width // 2), BF16),
            struct((rows, half), F32),
            struct((rows, half), F32),
        ],
        prefetch=1,
        flops=2 * rows * width * (rows + wide),
        moved=6 * rows * width + 2 * width * wide + 4 * rows * wide,
    )(place, landing_row, arrived, gain, w_branch, w_input)


def tile_scan(rates, drives, keep_in, state_in, reverse):
    rows, lanes = rates.shape
    groups = rows // GROUP
    a = rates.reshape(groups, GROUP, lanes)
    d = drives.reshape(groups, GROUP, lanes)
    spot = lax.broadcasted_iota(jnp.int32, (groups, GROUP, lanes), 1)
    for by in (1, 2, 4):
        turn = GROUP - by if reverse else by
        ok = spot < GROUP - by if reverse else spot >= by
        d_near = pltpu.roll(d, turn, 1)
        a_near = pltpu.roll(a, turn, 1)
        d = jnp.where(ok, a * d_near + d, d)
        a = jnp.where(ok, a * a_near, a)
    end = 0 if reverse else GROUP - 1
    keeps, states = [None] * groups, [None] * groups
    for g in range(groups - 1, -1, -1) if reverse else range(groups):
        keeps[g] = a[g] * keep_in
        states[g] = d[g] + a[g] * state_in
        keep_in = keeps[g][end : end + 1]
        state_in = states[g][end : end + 1]
    return jnp.concatenate(keeps, 0), jnp.concatenate(states, 0), keep_in, state_in


def recurrent_forward(inputs, halo, dist, conv_weight, conv_bias, decay, gate_weights):
    rows, width = inputs.shape
    tile = 256
    last = rows // tile - 1

    def body(
        in_ref, halo_ref, dist_ref, cw_ref, cb_ref, dp_ref, gw_ref,
        conv_ref, pre_ref, keep_ref, prefix_ref, local_ref, tail_ref,
        ext, carry,
    ):
        i = pl.program_id(0)

        @pl.when(i == 0)
        def _():
            ext[0:8] = halo_ref[...]
            carry[0:1] = jnp.ones((1, width), F32)
            carry[1:2] = jnp.zeros((1, width), F32)

        @pl.when(i > 0)
        def _():
            ext[0:8] = ext[tile : tile + 8]

        ext[8 : 8 + tile] = in_ref[...]
        dist = dist_ref[...]
        conv = cb_ref[...] + cw_ref[0:1] * ext[8 : 8 + tile]
        for k in range(1, CONV):
            conv = conv + jnp.where(dist >= k, cw_ref[k : k + 1] * ext[8 - k : 8 - k + tile], 0.0)
        conv_low = conv.astype(BF16)
        conv_ref[...] = conv_low
        pre_ref[...] = mm(conv_low, gw_ref[...])
        notstart = dist > 0
        for lane in range(0, width, LANES):
            cut = slice(lane, lane + LANES)
            far = slice(width + lane, width + lane + LANES)
            reset = sigmoid(pre_ref[:, cut])
            gate = sigmoid(pre_ref[:, far])
            keep = jnp.exp((-GATE_POWER * softplus_neg(dp_ref[:, cut])) * reset)
            drive = jnp.sqrt(1.0 - keep * keep + ROOT_FLOOR) * (gate * conv_ref[:, cut].astype(F32))
            rate = jnp.where(notstart, keep, 0.0)
            keep_ref[:, cut] = rate
            keeps, states, keep_out, state_out = tile_scan(
                rate, drive, carry[0:1, cut], carry[1:2, cut], False
            )
            prefix_ref[:, cut] = keeps
            local_ref[:, cut] = states
            carry[0:1, cut] = keep_out
            carry[1:2, cut] = state_out

        @pl.when(i == last)
        def _():
            tail_ref[...] = carry[...]

    tiles = pl.BlockSpec((tile, width), lambda i: (i, 0))
    return call(
        body,
        (rows // tile,),
        [
            tiles,
            whole((8, width)),
            pl.BlockSpec((tile, 1), lambda i: (i, 0)),
            whole((CONV, width)),
            whole((1, width)),
            whole((1, width)),
            whole((width, 2 * width)),
        ],
        [
            tiles,
            pl.BlockSpec((tile, 2 * width), lambda i: (i, 0)),
            tiles,
            tiles,
            tiles,
            whole((8, width)),
        ],
        [
            struct((rows, width), BF16),
            struct((rows, 2 * width), F32),
            struct((rows, width), F32),
            struct((rows, width), F32),
            struct((rows, width), F32),
            struct((8, width), F32),
        ],
        [pltpu.VMEM((tile + 8, width), F32), pltpu.VMEM((8, width), F32)],
        flops=4 * rows * width * width + 200 * rows * width,
        moved=30 * rows * width,
    )(inputs, halo, dist, conv_weight, conv_bias, decay, gate_weights)


def finish_states(place, pieces, local, prefix, branch, owners):
    rows, width = local.shape
    shards = pieces.shape[0]
    tile = rows // owners // CHUNKS

    def body(my_ref, pieces_ref, local_ref, prefix_ref, branch_ref, states_ref, carry_ref, *mixed_refs):
        mine = my_ref[0]
        i = pl.program_id(0)

        @pl.when(i == 0)
        def _():
            entering = jnp.zeros((1, width), F32)
            for s in range(shards - 1):
                longer = pieces_ref[s, 0:1] * entering + pieces_ref[s, 1:2]
                entering = jnp.where(s < mine, longer, entering)
            carry_ref[...] = jnp.broadcast_to(entering, (8, width))

        states = local_ref[...] + prefix_ref[...] * carry_ref[0:1]
        states_ref[...] = states
        mixed = (states * gelu(branch_ref[...])).astype(BF16)
        for c in range(CHUNKS):

            @pl.when(i % CHUNKS == c)
            def _(c=c):
                mixed_refs[c][0] = mixed

    tiles = pl.BlockSpec((tile, width), lambda i, *_: (i, 0))
    return call(
        body,
        (rows // tile,),
        [whole(pieces.shape), tiles, tiles, tiles],
        [
            tiles,
            whole((8, width)),
        ]
        + [pl.BlockSpec((1, tile, width), lambda i, *_: (i // CHUNKS, 0, 0))] * CHUNKS,
        [struct((rows, width), F32), struct((8, width), F32)]
        + [struct((owners, tile, width), BF16)] * CHUNKS,
        prefetch=1,
        flops=60 * rows * width,
        moved=18 * rows * width,
    )(place, pieces, local, prefix, branch)


def output_rows(chunk, place, mixed_full, w_near, w_far, stream, gain, kept):
    sources, sub, width = mixed_full.shape
    own = sub * CHUNKS
    channels = w_near.shape[1]
    model = stream.shape[1]
    half = model // 2

    def body(place_ref, mixed_ref, near_ref, far_ref, stream_ref, gain_ref, *rest):
        resid_ref, rows_ref, normed_ref = rest[-3:]
        s = pl.program_id(0)
        rows_ref[...] = mixed_ref[0]
        near = pl.ds(pl.multiple_of(place_ref[2] * half, half), half)
        far = pl.ds(pl.multiple_of((1 - place_ref[2]) * half, half), half)

        @pl.when(s == 0)
        def _():
            resid_ref[...] = stream_ref[...].astype(F32)

        mixed = mixed_ref[0, :, :channels]
        resid_ref[:, near] += mm(mixed, near_ref[0])
        resid_ref[:, far] += mm(mixed, far_ref[0])

        @pl.when(s == sources - 1)
        def _():
            x = resid_ref[...]
            inv = lax.rsqrt(jnp.mean(x * x, axis=-1, keepdims=True) + EPSILON)
            normed_ref[...] = (x * inv * gain_ref[...]).astype(BF16)

    kept = tuple(kept)
    return call(
        body,
        (sources,),
        [
            pl.BlockSpec((1, sub, width), lambda s, *_: (s, 0, 0)),
            pl.BlockSpec((1, channels, half), lambda s, *_: (s, 0, 0)),
            pl.BlockSpec((1, channels, half), lambda s, *_: (s, 0, 0)),
            pl.BlockSpec((sub, model), lambda s, p: (p[1] * CHUNKS + chunk, 0)),
            whole((1, model)),
        ]
        + [pl.BlockSpec(memory_space=pl.ANY)] * len(kept),
        [
            pl.BlockSpec((sub, model), lambda s, *_: (chunk, 0)),
            pl.BlockSpec((sub, width), lambda s, *_: (chunk, s)),
            whole((sub, model)),
        ],
        [
            struct((own, model), F32),
            struct((own, sources * width), BF16),
            struct((sub, model), BF16),
        ],
        prefetch=1,
        aliases={6 + j: j for j in range(len(kept))},
        flops=2 * sources * sub * width * model,
        moved=2 * sources * width * model + 8 * sub * model,
    )(place, mixed_full, w_near, w_far, stream, gain, *kept)


def mlp_tile(hidden):
    return 256 if hidden % 256 == 0 else LANES


def mlp_chunk(chunk, place, normed, upstream, resid_own, w_gate, w_up, w_down, parts, kept):
    rows, model = normed.shape
    hidden = w_gate.shape[1]
    total = upstream.shape[0]
    sub = resid_own.shape[0] // CHUNKS
    tile = mlp_tile(hidden)
    steps = hidden // tile

    def body(place_ref, n_ref, u_ref, r_ref, wg_ref, wu_ref, wd_ref, *rest):
        act_ref, pair_ref, near_ref, far_ref, down_ref, grad_ref, down_acc, grad_acc = rest[-8:]
        s = pl.program_id(0)

        @pl.when(s == 0)
        def _():
            split_columns(near_ref, far_ref, n_ref[...], place_ref[2], parts)
            down_acc[...] = jnp.zeros_like(down_acc)
            own = pl.ds(pl.multiple_of(place_ref[1] * sub, sub), sub)
            down_acc[own, :] = r_ref[...]

        gate_pre = mm(n_ref[...], wg_ref[...])
        up_pre = mm(n_ref[...], wu_ref[...])
        inner = mm(u_ref[...], wd_ref[...], NT)
        act, slope = gelu_both(gate_pre)
        inner_act = (act * up_pre).astype(BF16)
        gate_low = (inner * up_pre * slope).astype(BF16)
        up_low = (inner * act).astype(BF16)
        act_ref[...] = inner_act
        pair_ref[:, :tile] = gate_low
        pair_ref[:, tile:] = up_low
        down_acc[...] += mm(inner_act, wd_ref[...])
        both = mm(gate_low, wg_ref[...], NT) + mm(up_low, wu_ref[...], NT)

        @pl.when(s == 0)
        def _():
            grad_acc[...] = both

        @pl.when(s > 0)
        def _():
            grad_acc[...] += both

        @pl.when(s == steps - 1)
        def _():
            down_ref[...] = down_acc[...].astype(BF16)
            grad_ref[...] = grad_acc[...].astype(BF16)

    rows_of = pl.BlockSpec((rows, model), lambda s, *_: (chunk, 0))
    kept = tuple(kept)
    return call(
        body,
        (steps,),
        [
            whole((rows, model)),
            rows_of,
            pl.BlockSpec((sub, model), lambda s, *_: (chunk, 0)),
            pl.BlockSpec((model, tile), lambda s, *_: (0, s)),
            pl.BlockSpec((model, tile), lambda s, *_: (0, s)),
            pl.BlockSpec((tile, model), lambda s, *_: (s, 0)),
        ]
        + [pl.BlockSpec(memory_space=pl.ANY)] * len(kept),
        [
            pl.BlockSpec((rows, tile), lambda s, *_: (chunk, s)),
            pl.BlockSpec((rows, 2 * tile), lambda s, *_: (chunk, s)),
            pl.BlockSpec((rows, model // 2), lambda s, *_: (chunk, 0)),
            pl.BlockSpec((rows, model // 2), lambda s, *_: (chunk, 0)),
            rows_of,
            whole((rows, model)),
        ],
        [
            struct((total, hidden), BF16),
            struct((total, 2 * hidden), BF16),
            struct((total, model // 2), BF16),
            struct((total, model // 2), BF16),
            struct((total, model), BF16),
            struct((rows, model), BF16),
        ],
        [pltpu.VMEM((rows, model), F32), pltpu.VMEM((rows, model), F32)],
        prefetch=1,
        aliases={7 + j: j for j in range(len(kept))},
        flops=12 * rows * hidden * model,
        moved=6 * hidden * model + 10 * rows * model,
    )(place, normed, upstream, resid_own, w_gate, w_up, w_down, *kept)


def resid_backward(chunk, place, normed_grad, upstream, resid_own, gain, w_near, w_far, width, parts, kept):
    sub, model = normed_grad.shape
    own = resid_own.shape[0]
    sources, channels, half = w_near.shape

    def body(place_ref, g_ref, up_ref, r_ref, gain_ref, near_ref, far_ref, *rest):
        low_near_ref, low_far_ref, rg_ref, mg_ref, sum_ref, low_ref = rest[-6:]

        @pl.when(pl.program_id(0) == 0)
        def _():
            x = r_ref[...]
            g = g_ref[...].astype(F32)
            inv = lax.rsqrt(jnp.mean(x * x, axis=-1, keepdims=True) + EPSILON)
            unit = x * inv
            scaled = g * gain_ref[...]
            dot = jnp.mean(scaled * unit, axis=-1, keepdims=True)
            grad = up_ref[...].astype(F32) + inv * (scaled - unit * dot)
            rg_ref[...] = grad
            low_ref[...] = grad.astype(BF16)
            split_columns(low_near_ref, low_far_ref, grad.astype(BF16), place_ref[2], parts)
            sum_ref[...] = jnp.sum(g * unit, axis=0, keepdims=True)

        near = pl.ds(pl.multiple_of(place_ref[2] * half, half), half)
        far = pl.ds(pl.multiple_of((1 - place_ref[2]) * half, half), half)
        if channels < width:
            mg_ref[...] = jnp.zeros_like(mg_ref)
        mg_ref[0, :, :channels] = (
            mm(low_ref[:, near], near_ref[0], NT) + mm(low_ref[:, far], far_ref[0], NT)
        ).astype(BF16)

    rows = pl.BlockSpec((sub, model), lambda s, *_: (chunk, 0))
    kept = tuple(kept)
    return call(
        body,
        (sources,),
        [
            whole((sub, model)),
            pl.BlockSpec((sub, model), lambda s, p: (chunk * sources + p[1], 0)),
            rows,
            whole((1, model)),
            pl.BlockSpec((1, channels, half), lambda s, *_: (s, 0, 0)),
            pl.BlockSpec((1, channels, half), lambda s, *_: (s, 0, 0)),
        ]
        + [pl.BlockSpec(memory_space=pl.ANY)] * len(kept),
        [
            pl.BlockSpec((sub, half), lambda s, *_: (chunk, 0)),
            pl.BlockSpec((sub, half), lambda s, *_: (chunk, 0)),
            rows,
            pl.BlockSpec((1, sub, width), lambda s, *_: (s, chunk, 0)),
            whole((1, model)),
        ],
        [
            struct((own, half), BF16),
            struct((own, half), BF16),
            struct((own, model), F32),
            struct((sources, own, width), BF16),
            struct((1, model), F32),
        ],
        [pltpu.VMEM((sub, model), BF16)],
        prefetch=1,
        aliases={7 + j: j for j in range(len(kept))},
        flops=2 * sources * sub * width * model,
        moved=2 * sources * width * model + 14 * sub * model,
    )(place, normed_grad, upstream, resid_own, gain, w_near, w_far, *kept)


def recurrent_back_scan(mixed_grad, branch, keep, tail):
    rows, width = branch.shape
    tile = 256
    tiles_n = rows // tile

    def body(mg_ref, branch_ref, keep_ref, tail_ref, grad_ref, after_ref, edge_ref, ext, carry):
        i = pl.program_id(0)

        @pl.when(i == 0)
        def _():
            ext[tile : tile + 8] = jnp.ones((8, width), F32)
            carry[0:1] = jnp.ones((1, width), F32)
            carry[1:2] = jnp.zeros((1, width), F32)

        @pl.when(i > 0)
        def _():
            ext[tile : tile + 8] = ext[0:8]

        ext[0:tile] = keep_ref[...]
        for lane in range(0, width, LANES):
            cut = slice(lane, lane + LANES)
            direct = mg_ref[:, cut].astype(F32) * gelu(branch_ref[:, cut])
            keeps, grads, keep_out, grad_out = tile_scan(
                ext[1 : tile + 1, cut], direct, carry[0:1, cut], carry[1:2, cut], True
            )
            grad_ref[:, cut] = grads
            after_ref[:, cut] = keeps
            carry[0:1, cut] = keep_out
            carry[1:2, cut] = grad_out

        @pl.when(i == tiles_n - 1)
        def _():
            edge_ref[0:1] = tail_ref[0:1]
            edge_ref[1:2] = keep_ref[0:1] * carry[1:2]
            edge_ref[2:8] = jnp.zeros((6, width), F32)

    tiles = pl.BlockSpec((tile, width), lambda i: (tiles_n - 1 - i, 0))
    return call(
        body,
        (tiles_n,),
        [tiles, tiles, tiles, whole((8, width))],
        [tiles, tiles, whole((8, width))],
        [struct((rows, width), F32), struct((rows, width), F32), struct((8, width), F32)],
        [pltpu.VMEM((tile + 8, width), F32), pltpu.VMEM((8, width), F32)],
        flops=100 * rows * width,
        moved=18 * rows * width,
    )(mixed_grad, branch, keep, tail)


def recurrent_backward(
    place, pieces, local_grad, after_keep, mixed_grad, branch, states, carry_in, pre, conv_low,
    dist, inputs, halo, conv_weight, decay, gate_weights,
):
    rows, width = branch.shape
    shards = pieces.shape[0]
    tile = 256
    tiles_n = rows // tile
    blocks = tile // 8

    def body(
        place_ref, pieces_ref, lg_ref, ak_ref, mg_ref, branch_ref, states_ref, before_ref, carry_ref,
        pre_ref, conv_ref, dist_ref, in_ref, in_before_ref, halo_ref, cw_ref, dp_ref, gw_ref,
        bl_ref, il_ref, pl_ref, sums_ref, end_ref, edge_ref,
        back, prev, ext, acc, cg,
    ):
        i = pl.program_id(0)
        mine = place_ref[0]

        @pl.when(i == 0)
        def _():
            entering = jnp.zeros((1, width), F32)
            for s in range(shards - 1, 0, -1):
                longer = pieces_ref[s, 0:1] * entering + pieces_ref[s, 1:2]
                entering = jnp.where(s > mine, longer, entering)
            back[...] = jnp.broadcast_to(entering, (8, width))
            sums_ref[...] = jnp.zeros_like(sums_ref)
            acc[tile : tile + 16] = jnp.zeros((16, width), F32)

        @pl.when(i > 0)
        def _():
            acc[tile : tile + 8] = acc[0:8]
            acc[tile + 8 : tile + 16] = jnp.zeros((8, width), F32)

        @pl.when(i == tiles_n - 1)
        def _():
            prev[0:8] = carry_ref[...]
            ext[0:8] = halo_ref[...]

        @pl.when(i < tiles_n - 1)
        def _():
            prev[0:8] = before_ref[...]
            ext[0:8] = in_before_ref[...]

        prev[8 : 8 + tile] = states_ref[...]
        ext[8 : 8 + tile] = in_ref[...]
        acc[0:tile] = jnp.zeros((tile, width), F32)
        dist = dist_ref[...]
        notstart = dist > 0
        for lane in range(0, width, LANES):
            cut = slice(lane, lane + LANES)
            far = slice(width + lane, width + lane + LANES)
            grad = lg_ref[:, cut] + ak_ref[:, cut] * back[0:1, cut]
            _, slope = gelu_both(branch_ref[:, cut])
            bl_ref[:, cut] = (mg_ref[:, cut].astype(F32) * states_ref[:, cut] * slope).astype(BF16)
            reset = sigmoid(pre_ref[:, cut])
            gate = sigmoid(pre_ref[:, far])
            power = -GATE_POWER * softplus_neg(dp_ref[:, cut])
            keep = jnp.exp(power * reset)
            inside = 1.0 - keep * keep + ROOT_FLOOR
            unroot = lax.rsqrt(inside)
            root = inside * unroot
            conv = conv_ref[:, cut].astype(F32)
            through = gate * conv
            keep_grad = jnp.where(notstart, grad * prev[7 : 7 + tile, cut], 0.0) - grad * through * (
                keep * unroot
            )
            kg = keep_grad * keep * reset
            pl_ref[:, cut] = (kg * power * (1.0 - reset)).astype(BF16)
            rooted = grad * root
            cg[:, cut] = rooted * gate
            pl_ref[:, far] = (rooted * through * (1.0 - gate)).astype(BF16)
            sums_ref[40:48, cut] += jnp.sum(kg.reshape(blocks, 8, LANES), axis=0)
        cg[...] += mm(pl_ref[...], gw_ref[...], NT)
        for lane in range(0, width, LANES):
            cut = slice(lane, lane + LANES)
            conv_grad = cg[:, cut]
            sums_ref[32:40, cut] += jnp.sum(conv_grad.reshape(blocks, 8, LANES), axis=0)
            for k in range(CONV):
                masked = conv_grad if k == 0 else jnp.where(dist >= k, conv_grad, 0.0)
                tap = masked * ext[8 - k : 8 - k + tile, cut]
                sums_ref[8 * k : 8 * k + 8, cut] += jnp.sum(tap.reshape(blocks, 8, LANES), axis=0)
                acc[8 - k : 8 - k + tile, cut] += cw_ref[k : k + 1, cut] * masked
        il_ref[...] = acc[8 : 8 + tile].astype(BF16)

        @pl.when(i == 0)
        def _():
            end_ref[...] = acc[tile : tile + 8]

        @pl.when(i == tiles_n - 1)
        def _():
            edge_ref[...] = acc[0:8]

    tiles = pl.BlockSpec((tile, width), lambda i, *_: (tiles_n - 1 - i, 0))
    wide = pl.BlockSpec((tile, 2 * width), lambda i, *_: (tiles_n - 1 - i, 0))
    before = pl.BlockSpec(
        (8, width), lambda i, *_: (jnp.maximum((tiles_n - 1 - i) * blocks - 1, 0), 0)
    )
    small = whole((8, width))
    return call(
        body,
        (tiles_n,),
        [
            whole(pieces.shape), tiles, tiles, tiles, tiles, tiles, before, small, wide, tiles,
            pl.BlockSpec((tile, 1), lambda i, *_: (tiles_n - 1 - i, 0)),
            tiles, before, small, whole((CONV, width)), whole((1, width)), whole((width, 2 * width)),
        ],
        [tiles, tiles, wide, whole((48, width)), small, small],
        [
            struct((rows, 2 * width), BF16),
            struct((rows, width), BF16),
            struct((rows, 2 * width), BF16),
            struct((48, width), F32),
            struct((8, width), F32),
            struct((8, width), F32),
        ],
        [
            pltpu.VMEM((8, width), F32),
            pltpu.VMEM((tile + 8, width), F32),
            pltpu.VMEM((tile + 8, width), F32),
            pltpu.VMEM((tile + 16, width), F32),
            pltpu.VMEM((tile, width), F32),
        ],
        prefetch=1,
        flops=4 * rows * width * width + 300 * rows * width,
        moved=40 * rows * width,
    )(
        place, pieces, local_grad, after_keep, mixed_grad, branch, states, states, carry_in, pre,
        conv_low, dist, inputs, inputs, halo, conv_weight, decay, gate_weights,
    )


def input_backward(place, rec_low, inputs_low, end, returned, w_branch, w_input, stream, gain, resid_grad):
    rows, width = inputs_low.shape
    channels = w_branch.shape[0]
    model = stream.shape[1]
    tile = resid_grad.shape[0]
    steps = rows // tile

    def body(
        place_ref, bl_ref, il_ref, end_ref, ret_ref, wb_ref, wi_ref, x_ref, gain_ref, rg_ref,
        part_ref, fixed_ref, sum_ref,
    ):
        i = pl.program_id(0)
        fixed_ref[...] = il_ref[...]

        @pl.when(i == steps - 1)
        def _():
            tail = jnp.concatenate(
                [il_ref[tile - 16 : tile - 8].astype(F32), end_ref[...] + ret_ref[...]], axis=0
            )
            fixed_ref[tile - 16 : tile] = tail.astype(BF16)

        g = mm(bl_ref[:, :channels], wb_ref[...]) + mm(fixed_ref[:, :channels], wi_ref[...])
        x = x_ref[...].astype(F32)
        inv = lax.rsqrt(jnp.mean(x * x, axis=-1, keepdims=True) + EPSILON)
        unit = x * inv
        scaled = g * gain_ref[...]
        dot = jnp.mean(scaled * unit, axis=-1, keepdims=True)
        part = inv * (scaled - unit * dot)
        sums = jnp.sum(g * unit, axis=0, keepdims=True)

        @pl.when(i == 0)
        def _():
            sum_ref[...] = sums

        @pl.when(i > 0)
        def _():
            sum_ref[...] += sums

        @pl.when(i == place_ref[1])
        def _():
            part_ref[...] = (part + rg_ref[...]).astype(BF16)

        @pl.when(i != place_ref[1])
        def _():
            part_ref[...] = part.astype(BF16)

    tiles = pl.BlockSpec((tile, width), lambda i, *_: (i, 0))
    wide = pl.BlockSpec((tile, model), lambda i, *_: (i, 0))
    return call(
        body,
        (steps,),
        [
            tiles, tiles, whole((8, width)), whole((8, width)), whole((channels, model)), whole((channels, model)), wide,
            whole((1, model)), whole((tile, model)),
        ],
        [wide, pl.BlockSpec((tile, width), lambda i, *_: (i, 1)), whole((1, model))],
        [struct((rows, model), BF16), struct((rows, 2 * width), BF16), struct((1, model), F32)],
        prefetch=1,
        aliases={1: 1},
        flops=4 * rows * width * model + 30 * rows * model,
        moved=4 * rows * model + 4 * width * model + 6 * rows * width,
    )(place, rec_low, inputs_low, end, returned, w_branch, w_input, stream, gain, resid_grad)


def gate_gradients(conv_low, pre_low, extra, heads):
    rows, width = conv_low.shape
    size = extra.shape[0]

    def body(conv_ref, pre_ref, extra_ref, out_ref, full):
        full[...] = mm(conv_ref[...], pre_ref[...], TN)
        for g in range(2):
            for h in range(heads):
                at = h * size
                out_ref[g * heads + h] = full[at : at + size, g * width + at : g * width + at + size]
        out_ref[2 * heads] = extra_ref[...]

    return call(
        body,
        (1,),
        [whole((rows, width)), whole((rows, 2 * width)), whole((size, size))],
        whole((2 * heads + 1, size, size)),
        struct((2 * heads + 1, size, size), F32),
        [pltpu.VMEM((width, 2 * width), F32)],
        flops=4 * rows * width * width,
        moved=6 * rows * width,
    )(conv_low, pre_low, extra)


def block_diagonal(blocks, width):
    heads, size = blocks.shape[0], blocks.shape[1]
    rows = [
        jnp.pad(blocks[h], ((0, 0), (h * size, width - (h + 1) * size))) for h in range(heads)
    ]
    return jnp.pad(jnp.concatenate(rows, axis=0), ((0, width - heads * size), (0, 0)))


def shards(
    tokens,
    cotangent,
    destination,
    lengths,
    norm_gain,
    w_branch,
    w_input,
    conv_weight,
    conv_bias,
    w_recur,
    w_ingate,
    decay_param,
    w_out,
    mlp_gain,
    w_gate,
    w_up,
    w_down,
):
    shard_count = lax.axis_size("seq")
    my_shard = lax.axis_index("seq")
    model_count = lax.axis_size("mp")
    my_model = lax.axis_index("mp")
    row_count, model_width = tokens.shape
    slab_width = model_width // model_count
    per_peer = row_count // shard_count
    own_rows = row_count // model_count
    sub = own_rows // CHUNKS
    channels = w_branch.shape[1]
    heads, block_width = w_recur.shape[0], w_recur.shape[1]
    width = -(-channels // LANES) * LANES
    parity = my_shard % 2
    place = jnp.stack([my_shard, my_model, parity]).astype(jnp.int32)
    pad_lanes = functools.partial(jnp.pad, pad_width=((0, 0), (0, width - channels)))

    bits = shard_count.bit_length() - 1

    def scatter_sum(x, axis, dim):
        return lax.psum_scatter(x, axis, scatter_dimension=dim, tiled=True)

    def exchange(x, axis):
        return lax.all_to_all(x, axis, split_axis=0, concat_axis=0, tiled=True)

    def swap(x, bit):
        return lax.ppermute(x, "seq", [(i, i ^ (1 << bit)) for i in range(shard_count)])

    def add_low(left, right):
        return (left.astype(F32) + right.astype(F32)).astype(BF16)

    def tie(*values):
        return lax.optimization_barrier(values)

    def halves(x, up):
        done = bits - x.shape[0].bit_length() + 1
        bit = done if up else bits - done
        mine = (my_shard >> bit) & 1
        axis = 1 if up else 0
        x = x.reshape(-1, 2, *x.shape[1:]) if up else x.reshape(2, -1, *x.shape[1:])
        return bit, [lax.dynamic_index_in_dim(x, m, axis, False) for m in (mine, 1 - mine)]

    def others(pair):
        return [halves(x, up)[1][1] for x, up in zip(pair, (True, False))]

    def send_others(pair, made):
        return [swap(o, halves(x, up)[0]) for x, up, o in zip(pair, (True, False), made)]

    def send_all(pair):
        return send_others(pair, others(pair))

    def add_all(pair, received):
        return [add_low(halves(x, up)[1][0], r) for x, up, r in zip(pair, (True, False), received)]

    local_dest = lax.dynamic_slice_in_dim(destination, my_shard * row_count, row_count)
    dest_row, dest_col = local_dest.reshape(1, -1), local_dest.reshape(-1, 1)
    straight = jnp.zeros((1,), jnp.int32)
    turn = (my_shard * per_peer).astype(jnp.int32)[None]
    w_gates = jnp.concatenate(
        [block_diagonal(w_recur, width), block_diagonal(w_ingate, width)], axis=1
    )
    sent_tokens, w_gates, cotangent = tie(
        send_order(straight, dest_row, dest_col, tokens), w_gates, cotangent
    )
    arrived_tokens = exchange(sent_tokens, "seq")
    cot_blocks = send_blocks(turn, dest_row, dest_col, cotangent, shard_count)
    sorted_dest = jnp.sort(destination.reshape(shard_count, row_count), axis=1)
    landing = (
        lax.dynamic_slice_in_dim(sorted_dest, my_shard * per_peer, per_peer, 1).reshape(-1)
        - my_shard * row_count
    )
    landing_row = landing.reshape(1, -1)
    turned = jnp.stack(
        [
            lax.dynamic_index_in_dim(landing.reshape(shard_count, per_peer), my_shard ^ k, 0, False)
            for k in range(shard_count)
        ]
    ).reshape(1, -1)
    cot_other = swap(jnp.concatenate(cot_blocks[1::2], axis=0), 0).reshape(-1, per_peer, model_width)
    sent_cot = [
        jnp.concatenate([cot_blocks[2 * q], cot_other[q]], axis=0) for q in range(shard_count // 2)
    ]
    mlp_place = np.arange(row_count, dtype=np.int32).reshape(model_count, CHUNKS, sub)
    mlp_place = jnp.asarray(mlp_place.transpose(1, 0, 2).reshape(-1, 1))
    mlp_landing = (
        (landing % own_rows) // sub * (model_count * sub) + landing // own_rows * sub + landing % sub
    )

    positions = my_shard * row_count + jnp.arange(row_count, dtype=jnp.int32)
    count = lengths.shape[0]
    earlier = np.tril(np.ones((count, count), np.int32), -1)
    seq_starts = jnp.sum(jnp.asarray(earlier) * lengths[None, :], axis=1)
    seq_start = jnp.max(
        jnp.where(seq_starts[None, :] <= positions[:, None], seq_starts[None, :], 0), axis=1
    )
    dist = (positions - seq_start).reshape(-1, 1)

    w_branch, w_input = w_branch.T, w_input.T
    taps = pad_lanes(conv_weight)
    bias = pad_lanes(conv_bias[None])
    decay = pad_lanes(decay_param[None])
    gain = norm_gain[None]
    gain2 = mlp_gain[None]
    half = model_width // 2
    w_out_half = jnp.pad(
        lax.dynamic_slice_in_dim(w_out, parity * half, half, 1), ((0, -channels % 16), (0, 0))
    )
    w_near = lax.all_gather(w_out_half, "mp", axis=0)

    arrived_tokens, w_gates, *sent_cot = tie(arrived_tokens, w_gates, *sent_cot)
    stream, hidden_near, hidden_far, branch, inputs = project(
        place, landing_row, arrived_tokens, gain, w_branch, w_input, width, shard_count
    )
    halo = lax.ppermute(
        inputs[row_count - 8 :], "seq", [(i, i + 1) for i in range(shard_count - 1)]
    )
    conv_low, pre, keep, prefix, local, tail = recurrent_forward(
        inputs, halo, dist, taps, bias, decay, w_gates
    )
    pieces = lax.all_gather(tail, "seq")
    pieces, *sent_cot = tie(pieces, *sent_cot)
    cot_blocks = [sent_cot[0]] + [
        lax.ppermute(sent_cot[q], "seq", [(i, i ^ (2 * q)) for i in range(shard_count)])
        for q in range(1, shard_count // 2)
    ]
    states, carry_in, *mixed = finish_states(
        place, pieces, local, prefix, branch, model_count
    )
    mixed[0], w_near = tie(mixed[0], w_near)
    w_far = swap(w_near, 0)

    rows_kept, normeds = (), []
    for c in range(CHUNKS):
        mixed_full = exchange(mixed[c], "mp")
        if c == 0:
            mixed_full, *cot_blocks[1:3] = tie(mixed_full, *cot_blocks[1:3])
        *rows_kept, normed_own = output_rows(
            c, place, mixed_full, w_near, w_far, stream, gain2, rows_kept
        )
        normeds.append(normed_own)
    resid_own, mixed_rows = rows_kept
    normeds[-1], *cot_blocks = tie(normeds[-1], *cot_blocks)
    upstream, upstream_near, upstream_far = place_upstream(
        place, mlp_place, turned, cot_blocks, shard_count
    )
    kept, grads = (), []
    for c in range(CHUNKS):
        if c == 0:
            normed = lax.all_gather(normeds[c], "mp", axis=0, tiled=True)
        else:
            normed = exchange(
                jnp.broadcast_to(normeds[c], (model_count, *normeds[c].shape)), "mp"
            ).reshape(-1, model_width)
        *kept, grad = mlp_chunk(
            c, place, normed, upstream, resid_own, w_gate, w_up, w_down, shard_count, kept
        )
        grads.append(scatter_sum(grad, "mp", 0))
    inner_act, pair_low, normed_near, normed_far, block_part = kept

    parts = shard_count // 2
    part_width = model_width // shard_count
    hidden_units = w_gate.shape[1]

    def outer(left, right):
        return mm(left, right, TN).astype(BF16)

    def with_partner(near, sent, right):
        return (mm(near, right, TN) + sent.astype(F32)).astype(BF16).reshape(
            parts, part_width, right.shape[1]
        )

    def two_ways(x):
        cut = x.shape[2] // 2
        return [x[..., :cut], x[..., cut:]]

    def finish(pair):
        while pair[0].shape[0] > 1:
            pair = add_all(pair, send_all(pair))
        return jnp.concatenate([x[0] for x in pair], axis=1)

    far_pair = outer(normed_far, pair_low)
    far_down = outer(upstream_far, inner_act)
    grads[0], far_pair, far_down = tie(grads[0], far_pair, far_down)
    far_pair, far_down = swap(far_pair, 0), swap(far_down, 0)

    def second_norm(c, kept):
        return resid_backward(
            c, place, grads[c], upstream, resid_own, gain2, w_near, w_far, width, shard_count, kept
        )

    *lows, gain_first = second_norm(0, ())
    lows[0], pair_low = tie(lows[0], pair_low)
    grad_pair = with_partner(normed_near, far_pair, pair_low)
    grad_pair, inner_act = tie(grad_pair, inner_act)
    pair = two_ways(grad_pair)
    pair_received = send_all(pair)
    down = two_ways(with_partner(upstream_near, far_down, inner_act))
    grads[1], *down = tie(grads[1], *down)
    near_low, far_low, resid_grad, mixed_grad_full, gain_second = second_norm(1, lows)
    mlp_gain_part = gain_first + gain_second
    mixed_grad = exchange(mixed_grad_full.reshape(row_count, width), "mp")
    far_out = outer(far_low, mixed_rows)
    far_out, *pair_received = tie(far_out, *pair_received)
    pair = add_all(pair, pair_received)
    pair_received = send_all(pair)
    mixed_grad, far_out, block_part, *pair_received = tie(
        mixed_grad, far_out, block_part, *pair_received
    )
    far_out = swap(far_out, 0)
    block_share = scatter_sum(block_part, "mp", 1)

    local_grad, after_keep, edge_pair = recurrent_back_scan(mixed_grad, branch, keep, tail)
    back_pieces = lax.all_gather(edge_pair, "seq")
    back_pieces, *down = tie(back_pieces, *down)
    down_received = send_all(down)
    rec_low, inputs_part, pre_low, sums, end, edge = recurrent_backward(
        place, back_pieces, local_grad, after_keep, mixed_grad, branch, states, carry_in, pre,
        conv_low, dist, inputs, halo, taps, decay, w_gates,
    )
    edge, far_out, near_low, *down_received = tie(edge, far_out, near_low, *down_received)
    returned = lax.ppermute(edge, "seq", [(i + 1, i) for i in range(shard_count - 1)])
    out = two_ways(with_partner(near_low, far_out, mixed_rows))
    out_others = others(out)
    returned, out, out_others = tie(returned, out, out_others)
    out_received = send_others(out, out_others)
    input_part, rec_low, norm_gain_part = input_backward(
        place, rec_low, inputs_part, end, returned, w_branch, w_input, stream, gain, resid_grad
    )
    input_part, block_share, pre_low, pair, down, pair_received, down_received = tie(
        input_part, block_share, pre_low, pair, down, pair_received, down_received
    )
    input_share = scatter_sum(input_part, "mp", 1)

    far_rec = outer(hidden_far, rec_low)
    far_rec, pre_low, *out_received = tie(far_rec, pre_low, *out_received)
    far_rec = swap(far_rec, 0)
    all_rows = jnp.arange(row_count, dtype=jnp.int32)[None]
    home_block = exchange(place_rows(mlp_landing.reshape(-1, 1), all_rows, block_share), "seq")
    home_block, pre_low = tie(home_block, pre_low)

    sums = jnp.sum(sums.reshape(CONV + 2, 8, width), axis=1)[:, :channels]
    sums = jnp.concatenate(
        [sums[: CONV + 1], sums[CONV + 1 :] * (GATE_POWER * jax.nn.sigmoid(-decay_param))], axis=0
    )
    gains = jnp.concatenate([norm_gain_part, mlp_gain_part], axis=0)
    gains = gains.reshape(2, model_count, slab_width).transpose(1, 0, 2)
    gains = jnp.sum(exchange(gains, "mp"), axis=0)
    sum_rows = sums.size // block_width
    gain_rows = -(-gains.size // block_width)
    gains = jnp.pad(gains.reshape(-1), (0, gain_rows * block_width - gains.size))
    extra = jnp.concatenate(
        [sums.reshape(sum_rows, block_width), gains.reshape(gain_rows, block_width)], axis=0
    )
    extra = jnp.pad(extra, ((0, block_width - sum_rows - gain_rows), (0, 0)))
    small = gate_gradients(conv_low, pre_low, extra, heads)
    small, hidden_near = tie(small, hidden_near)
    small = lax.psum(small, "seq")
    sums = small[2 * heads, :sum_rows].reshape(CONV + 2, channels)
    gains = small[2 * heads, sum_rows : sum_rows + gain_rows].reshape(-1)
    gains = gains[: 2 * slab_width].reshape(2, slab_width)

    out = add_all(out, out_received)
    grad_rec = with_partner(hidden_near, far_rec, rec_low)
    rec = two_ways(grad_rec)
    rec_received = send_all(rec)
    sent_out = finish(out)
    sent_pair = finish(add_all(pair, pair_received))
    sent_down = finish(add_all(down, down_received)).astype(F32).T
    unit = mlp_tile(hidden_units)
    sent_pair = sent_pair.reshape(part_width, hidden_units // unit, 2, unit)
    sent_gate = sent_pair[:, :, 0].reshape(part_width, hidden_units).astype(F32)
    sent_up = sent_pair[:, :, 1].reshape(part_width, hidden_units).astype(F32)
    input_share, home_block, sent_gate, sent_up, sent_down = tie(
        input_share, home_block, sent_gate, sent_up, sent_down
    )
    input_share, sent_out = tie(input_share, sent_out)
    sent_out = scatter_sum(sent_out, "mp", 1)
    sent_out = sent_out[:, :channels].astype(F32).T

    home_input = exchange(place_rows(landing.reshape(-1, 1), all_rows, input_share), "seq")
    home_input, *rec_received = tie(home_input, *rec_received)
    sent_rec = finish(add_all(rec, rec_received))
    sent_branch = sent_rec[:, :channels].astype(F32)
    sent_input = sent_rec[:, width : width + channels].astype(F32)
    block_out = restore_rows(dest_row, dest_col, home_block)
    input_grad = restore_rows(dest_row, dest_col, home_input)
    return (
        block_out,
        input_grad,
        gains[0],
        sent_branch,
        sent_input,
        sums[:CONV],
        sums[CONV],
        small[:heads],
        small[heads : 2 * heads],
        sums[CONV + 1],
        sent_out,
        gains[1],
        sent_gate,
        sent_up,
        sent_down,
    )


def solution(mesh):
    in_specs = (
        P("seq", None),
        P("seq", None),
        P(),
        P(),
        P(),
        P(None, "mp"),
        P(None, "mp"),
        P(None, "mp"),
        P("mp"),
        P("mp", None, None),
        P("mp", None, None),
        P("mp"),
        P("mp", None),
        P(),
        P(None, "mp"),
        P(None, "mp"),
        P("mp", None),
    )
    out_specs = (
        P("seq", "mp"),
        P("seq", "mp"),
        P("mp"),
        P("seq", "mp"),
        P("seq", "mp"),
        P(None, "mp"),
        P("mp"),
        P("mp", None, None),
        P("mp", None, None),
        P("mp"),
        P("mp", "seq"),
        P("mp"),
        P("seq", "mp"),
        P("seq", "mp"),
        P("mp", "seq"),
    )
    return jax.shard_map(shards, mesh=mesh, in_specs=in_specs, out_specs=out_specs, check_vma=False)
```
